32 devices in a mesh: fsdp: 32 (over z, y, x, core).
Axes of the slice: x: 2, y: 2, z: 4, core: 2. Of those that a mesh axis runs over, the one named last changes fastest.
Arguments:
- tokens: bfloat16 [32768, 1024], P('fsdp'), may hold values from -6 to 6
- out_cotangent: bfloat16 [32768, 1024], P('fsdp'), may hold values from -6 to 6
- seq_lengths: int32 [128], replicated, may hold values from 0 to 1024, as said below
- seq_device: int32 [128], replicated, may hold values from 0 to 31, as said below
- seq_offset: int32 [128], replicated, may hold values from 0 to 1024, as said below
- ln1_gain: bfloat16 [1024], P('fsdp'), may hold values from 0.25 to 1.75
- ln1_bias: bfloat16 [1024], P('fsdp'), may hold values from -3 to 3
- qkv_weight: bfloat16 [1024, 3072], P('fsdp'), may hold values from -0.1875 to 0.1875
- qkv_bias: bfloat16 [3072], P('fsdp'), may hold values from -3 to 3
- dense_weight: bfloat16 [1024, 1024], P('fsdp'), may hold values from -1 to 1
- dense_bias: bfloat16 [1024], P('fsdp'), may hold values from -3 to 3
- ln2_gain: bfloat16 [1024], P('fsdp'), may hold values from 0.25 to 1.75
- ln2_bias: bfloat16 [1024], P('fsdp'), may hold values from -3 to 3
- fc1_weight: bfloat16 [1024, 4096], P('fsdp'), may hold values from -0.1875 to 0.1875
- fc1_bias: bfloat16 [4096], P('fsdp'), may hold values from -3 to 3
- fc2_weight: bfloat16 [4096, 1024], P('fsdp'), may hold values from -0.09375 to 0.09375
- fc2_bias: bfloat16 [1024], P('fsdp'), may hold values from -3 to 3
Outputs:
- output: bfloat16 [32768, 1024], P('fsdp')
- grad_tokens: bfloat16 [32768, 1024], P('fsdp')
- grad_ln1_gain: float32 [1024], P('fsdp')
- grad_ln1_bias: float32 [1024], P('fsdp')
- grad_qkv_weight: float32 [1024, 3072], P('fsdp')
- grad_qkv_bias: float32 [3072], P('fsdp')
- grad_dense_weight: float32 [1024, 1024], P('fsdp')
- grad_dense_bias: float32 [1024], P('fsdp')
- grad_ln2_gain: float32 [1024], P('fsdp')
- grad_ln2_bias: float32 [1024], P('fsdp')
- grad_fc1_weight: float32 [1024, 4096], P('fsdp')
- grad_fc1_bias: float32 [4096], P('fsdp')
- grad_fc2_weight: float32 [4096, 1024], P('fsdp')
- grad_fc2_bias: float32 [1024], P('fsdp')
The draws below stay inside these ranges and needn't reach their ends.
Inputs may be any that keep to these rules, and one draw needn't show every extreme that they name: `seq_lengths`: the sequences of one device block lie in order of their offsets without intersection within its 1024 rows; some device block holds a single sequence of exactly 1024 tokens; slots of length 0 occur. `seq_device`: every device block has exactly 4 sequence slots. `seq_offset`: A slot of length 0 may have offset 1024.
All inputs are finite; a program needn't handle non-finite values.
Results may differ from the reference program's by a relative error of at most 0.0078.
Values may be sent and summed in bfloat16 or wider, within the bound.
No kernel may reach another device: no remote copies, remote signals or barrier semaphores. Data moves between devices by JAX's collectives and lax.ppermute only.
A program may use at most 320 MiB of HBM per device.

```python
import math
import jax
import jax.numpy as jnp
from jax import lax

D = 1024
H = 16
HD = 64
ROT = 16
FF = 4096
TOK_DEV = 1024
SPD = 4
TOKENS = 32768
SEQS = 128
N_FSDP = 32


def seq_plan(key):
    devices_count = SEQS // SPD
    key_total, key_cut, key_forced, key_order = jax.random.split(key, 4)
    totals = jax.random.randint(key_total, (devices_count,), 3 * TOK_DEV // 8, TOK_DEV + 1)
    raw_cuts = jax.random.randint(key_cut, (devices_count, SPD - 1), 0, 1 << 30)
    cuts = jnp.sort(raw_cuts % (totals[:, None] + 1), axis=1)
    starts = jnp.concatenate([jnp.zeros((devices_count, 1), jnp.int32), cuts], axis=1)
    ends = jnp.concatenate([cuts, totals[:, None]], axis=1)
    lengths = ends - starts
    forced = jax.random.randint(key_forced, (), 0, devices_count)
    chosen = (jnp.arange(devices_count) == forced)[:, None]
    first_col = (jnp.arange(SPD) == 0)[None, :]
    lengths = jnp.where(chosen, jnp.where(first_col, TOK_DEV, 0), lengths)
    starts = jnp.where(chosen, jnp.where(first_col, 0, TOK_DEV), starts)
    owners = jnp.broadcast_to(jnp.arange(devices_count, dtype=jnp.int32)[:, None], (devices_count, SPD))
    order = jax.random.permutation(key_order, SEQS)
    return (lengths.reshape(-1)[order].astype(jnp.int32), owners.reshape(-1)[order].astype(jnp.int32), starts.reshape(-1)[order].astype(jnp.int32))


def draw_seq_lengths(key, part):
    lengths, owners, starts = seq_plan(key)
    return lengths


def draw_seq_device(key, part):
    lengths, owners, starts = seq_plan(key)
    return owners


def draw_seq_offset(key, part):
    lengths, owners, starts = seq_plan(key)
    return starts


def strengthened(entries, rng, source, target, shards_of, factor):
    owner, partner = [(jnp.arange(entries.shape[dim]) // (entries.shape[dim] // shards_of)).reshape([-1 if axis == dim else 1 for axis in range(entries.ndim)]) for dim in (source, target)]
    chosen = jax.random.permutation(rng, shards_of)[partner]
    strong = (owner == chosen) | (owner == (partner + shards_of // 2) % shards_of)
    return jnp.where(strong, factor * entries, entries)


def level_of(own_key, shape, shards, low, top_value):
    def one(dim, parts):
        draws = jax.random.uniform(jax.random.fold_in(jax.random.fold_in(own_key, 6), dim), (parts,), jnp.float32, low / len(shards), top_value / len(shards))
        return jnp.repeat(jnp.exp(draws), shape[dim] // parts).reshape((-1,) + (1,) * (len(shape) - dim - 1))

    loudness = one(*shards[0])
    for cut in shards[1:]:
        loudness = loudness * one(*cut)
    return loudness


def noise(rng, dims, scale, limit, cuts=(), kind=jnp.bfloat16):
    result = jax.random.normal(rng, dims, jnp.float32) * scale
    if len(cuts) > 0:
        result = level_of(rng, dims, cuts, -0.22, 0.18) * result
    return jnp.clip(result, min=-limit, max=limit).astype(kind)


def noise_with(stream_key, extent, scale, most, cuts, heavy, held_as=jnp.bfloat16):
    array = scale * jax.random.normal(stream_key, extent, jnp.float32)
    if cuts:
        array = array * level_of(stream_key, extent, cuts, -0.22, 0.18)
    return jnp.clip(strengthened(array, jax.random.fold_in(stream_key, 3), *heavy), -most, most).astype(held_as)


def setup_inputs(seed: int = 0) -> dict:
    keys = jax.random.split(jax.random.key(seed), 18)
    tokens = noise(keys[0], (TOKENS, D), 1.0, 6.0, ((0, 32),))
    out_cotangent = noise_with(keys[1], (TOKENS, D), 1.0, 6.0, ((0, 32),), (0, 1, 32, 2.75))
    seq_lengths = draw_seq_lengths(jax.random.fold_in(keys[17], 71), 0)
    seq_device = draw_seq_device(jax.random.fold_in(keys[17], 71), 0)
    seq_offset = draw_seq_offset(jax.random.fold_in(keys[17], 71), 0)
    ln1_gain = jnp.clip(1.0 + 0.15 * jax.random.normal(keys[5], (D,), jnp.float32), 0.25, 1.75).astype(jnp.bfloat16)
    ln1_bias = noise(keys[6], (D,), 0.3, 3.0, ((0, 32),))
    qkv_weight = noise(keys[7], (D, 3 * D), D ** -0.5, 0.1875, ((0, 32),))
    qkv_bias = noise(keys[8], (3 * D,), 0.3, 3.0, ((0, 32),))
    dense_weight = noise(keys[9], (D, D), (D // 32) ** -0.5, 1.0, ((0, 32),))
    dense_bias = noise(keys[10], (D,), 0.3, 3.0, ((0, 32),))
    ln2_gain = jnp.clip(1.0 + 0.15 * jax.random.normal(keys[11], (D,), jnp.float32), 0.25, 1.75).astype(jnp.bfloat16)
    ln2_bias = noise(keys[12], (D,), 0.3, 3.0, ((0, 32),))
    fc1_weight = noise(keys[13], (D, FF), D ** -0.5, 0.1875, ((0, 32),))
    fc1_bias = noise(keys[14], (FF,), 0.3, 3.0, ((0, 32),))
    fc2_weight = noise(keys[15], (FF, D), FF ** -0.5, 0.09375, ((0, 32),))
    fc2_bias = noise(keys[16], (D,), 0.3, 3.0, ((0, 32),))
    return dict(tokens=tokens, out_cotangent=out_cotangent, seq_lengths=seq_lengths, seq_device=seq_device, seq_offset=seq_offset, ln1_gain=ln1_gain, ln1_bias=ln1_bias, qkv_weight=qkv_weight, qkv_bias=qkv_bias, dense_weight=dense_weight, dense_bias=dense_bias, ln2_gain=ln2_gain, ln2_bias=ln2_bias, fc1_weight=fc1_weight, fc1_bias=fc1_bias, fc2_weight=fc2_weight, fc2_bias=fc2_bias)


EPSILON = 1e-05
MASKED = -1e+30

@jax.custom_vjp
def low(v):
    return lax.optimization_barrier(v.astype(jnp.bfloat16)).astype(jnp.float32)

@jax.custom_vjp
def low_back(v):
    return v

def low_keep(v):
    return (low(v), None)

def low_pass(kept, grad):
    return (grad,)

def back_keep(v):
    return (v, None)

def back_low(kept, grad):
    return (low(grad),)
low.defvjp(low_keep, low_pass)
low_back.defvjp(back_keep, back_low)

def layer_norm(values, gain_vec, bias_vec):
    row_mean = lax.optimization_barrier(jnp.mean(values, axis=-1, keepdims=True))
    centred = values - row_mean
    row_var = lax.optimization_barrier(jnp.mean(centred * centred, axis=-1, keepdims=True))
    return centred * lax.rsqrt(row_var + EPSILON) * gain_vec + bias_vec

def locate(lengths, device_of, offsets, rows, which):
    row_ids = jnp.arange(rows, dtype=jnp.int32)
    inside = ((device_of[None, :] == which) & (row_ids[:, None] >= offsets[None, :]) & (row_ids[:, None] < offsets[None, :] + lengths[None, :])).astype(jnp.int32)
    found_any = lax.optimization_barrier(jnp.sum(inside, axis=1))
    numbers = jnp.arange(lengths.shape[0], dtype=jnp.int32)
    segment = jnp.where(found_any > 0, lax.optimization_barrier(jnp.sum(inside * numbers[None, :], axis=1)), lengths.shape[0] + row_ids)
    position = jnp.where(found_any > 0, row_ids - lax.optimization_barrier(jnp.sum(inside * offsets[None, :], axis=1)), 0)
    return (segment.astype(jnp.int32), position.astype(jnp.int32))

def rotary_tables(position, head_dim, rotary):
    half_rot = rotary // 2
    exponent = jnp.arange(half_rot, dtype=jnp.float32) * (2.0 / rotary)
    frequency = jnp.exp(-math.log(10000.0) * exponent)
    angles = position.astype(jnp.float32)[:, None] * frequency[None, :]
    rest_dims = head_dim - rotary
    cosine = jnp.concatenate([jnp.cos(angles), jnp.cos(angles), jnp.ones((angles.shape[0], rest_dims), jnp.float32)], axis=1)
    sine_table = jnp.concatenate([jnp.sin(angles), jnp.sin(angles), jnp.zeros((angles.shape[0], rest_dims), jnp.float32)], axis=1)
    return (cosine, sine_table)

def rotate(values, cosine, sine_table, rotary):
    half_rot = rotary // 2
    turned = jnp.concatenate([-values[..., half_rot:rotary], values[..., :half_rot], values[..., rotary:]], axis=-1)
    return values * cosine[:, None, :] + turned * sine_table[:, None, :]

def block_layer(rows_in, param_set, segment, position):
    ln1_gain, ln1_bias, qkv_weight, qkv_bias, dense_weight, dense_bias, ln2_gain, ln2_bias, fc1_weight, fc1_bias, fc2_weight, fc2_bias = param_set
    highest = lax.Precision.HIGHEST
    rows = rows_in.shape[0]
    normed_one = low(layer_norm(rows_in, ln1_gain, ln1_bias))
    joined = low_back(jnp.dot(normed_one, qkv_weight, precision=highest) + qkv_bias)
    joined = joined.reshape(rows, 3, H, HD)
    cosine, sine_table = rotary_tables(position, HD, ROT)
    query = low(rotate(joined[:, 0], cosine, sine_table, ROT))
    keyed = low(rotate(joined[:, 1], cosine, sine_table, ROT))
    valued = low(joined[:, 2])
    raw_scores = low_back(jnp.einsum('qhd,khd->hqk', query, keyed, precision=highest))
    scores = raw_scores * HD ** (-0.5)
    row_ids = jnp.arange(rows)[:, None]
    col_ids = jnp.arange(rows)[None, :]
    allowed = (segment[:, None] == segment[None, :]) & (col_ids <= row_ids)
    scores = jnp.where(allowed[None], scores, MASKED)
    top_score = lax.optimization_barrier(jnp.max(scores, axis=-1, keepdims=True))
    expd = jnp.exp(scores - top_score)
    probs = expd / lax.optimization_barrier(jnp.sum(expd, axis=-1, keepdims=True))
    mixed = jnp.einsum('hqk,khd->qhd', low(probs), valued, precision=highest).reshape(rows, D)
    mixed = low(low_back(mixed))
    attn_out = jnp.dot(mixed, dense_weight, precision=highest) + dense_bias
    normed_two = low(layer_norm(rows_in, ln2_gain, ln2_bias))
    upper = low_back(jnp.dot(normed_two, fc1_weight, precision=highest) + fc1_bias)
    active = low(jax.nn.gelu(upper, approximate=False))
    mlp_out = jnp.dot(active, fc2_weight, precision=highest) + fc2_bias
    return rows_in + attn_out + mlp_out

def reference(tokens, out_cotangent, seq_lengths, seq_device, seq_offset, ln1_gain, ln1_bias, qkv_weight, qkv_bias, dense_weight, dense_bias, ln2_gain, ln2_bias, fc1_weight, fc1_bias, fc2_weight, fc2_bias):
    which_all = jnp.arange(N_FSDP, dtype=jnp.int32)
    segments, positions = lax.map(lambda which: locate(seq_lengths, seq_device, seq_offset, TOK_DEV, which), which_all)
    initials = (ln1_gain, ln1_bias, qkv_weight, qkv_bias, dense_weight, dense_bias, ln2_gain, ln2_bias, fc1_weight, fc1_bias, fc2_weight, fc2_bias)
    param_set = tuple((weight_arr.astype(jnp.float32) for weight_arr in initials))

    def forward(rows_all, params_now):

        def one_block(carried, inputs):
            return (carried, block_layer(inputs[0], params_now, inputs[1], inputs[2]))
        blocks = rows_all.reshape(N_FSDP, TOK_DEV, D)
        unused, results = lax.scan(jax.checkpoint(one_block), jnp.zeros((), jnp.float32), (blocks, segments, positions))
        return results.reshape(TOKENS, D)
    primal, pullback = jax.vjp(forward, tokens.astype(jnp.float32), param_set)
    grad_rows, grad_params = pullback(out_cotangent.astype(jnp.float32))
    return (primal.astype(jnp.bfloat16), grad_rows.astype(jnp.bfloat16), grad_params[0], grad_params[1], grad_params[2], grad_params[3], grad_params[4], grad_params[5], grad_params[6], grad_params[7], grad_params[8], grad_params[9], grad_params[10], grad_params[11])
```

```python
from functools import partial
import math

import jax
import jax.numpy as jnp
from jax import lax
from jax.experimental import pallas as pl
from jax.experimental.pallas import tpu as pltpu
from jax.sharding import PartitionSpec as P

D = 1024
H = 16
HD = 64
ROT = 16
FF = 4096

EPSILON = 1e-05
MASKED = -1e30
BF = jnp.bfloat16
F32 = jnp.float32
LAST = (((1,), (1,)), ((), ()))
FIRST = (((0,), (0,)), ((), ()))
VMEM_LIMIT = 60 * 1024 * 1024


def mm(a, b):
    return jnp.dot(a, b, preferred_element_type=F32)


def mm_last(a, b):
    return lax.dot_general(a, b, LAST, preferred_element_type=F32)


def mm_first(a, b):
    return lax.dot_general(a, b, FIRST, preferred_element_type=F32)


def assemble(w_scr, pieces, tab, base):
    for p, piece in enumerate(pieces):
        for j in range(8):
            w_scr[tab[base + p * 8 + j]] = piece[j, 0]


def put_rows(keep_ref, send_ref, tab, base, mine, tile, values):
    pairs = values.shape[0] // 64
    blocks = values.astype(BF).reshape(pairs, 2, 32, values.shape[1])
    even, odd = blocks[:, 0], blocks[:, 1]
    keep = jnp.where(mine == 0, even, odd)
    send = jnp.where(mine == 0, odd, even)
    for j in range(pairs):
        slot = tab[base + tile * pairs + j]
        keep_ref[slot, 0] = keep[j]
        send_ref[slot, 0] = send[j]


def turn(x, cosine, sine_a, sine_b, sign):
    left = pltpu.roll(x, x.shape[1] - ROT // 2, 1)
    right = pltpu.roll(x, ROT // 2, 1)
    return x * cosine - sign * (left * sine_a - right * sine_b)


TR = 1024
TG = 1024


def project_kernel(tab, n1, g, bias, cos, sa, sb, *refs):
    pa, pb, out, w_scr = refs[:4], refs[4:8], refs[8], refs[9]
    i = pl.program_id(0)
    from_b = (i == 1) | (i == 2)

    @pl.when(jnp.logical_not(from_b))
    def _():
        assemble(w_scr, pa, tab, 0)

    @pl.when(from_b)
    def _():
        assemble(w_scr, pb, tab, 32)

    def weight():
        return w_scr[...].reshape(D, D)

    @pl.when(i < 2)
    def _():
        def tile(t, carry):
            rows = pl.ds(t * TR, TR)
            val = mm(n1[rows, :], weight()) + bias[0].astype(F32)
            c, a, b = cos[rows, :], sa[rows, :], sb[rows, :]
            for j in range(D // 128):
                cols = slice(j * 128, j * 128 + 128)
                out[0, rows, cols] = turn(val[:, cols], c, a, b, 1.0).astype(BF)
            return carry

        lax.fori_loop(0, D // TR, tile, 0)

    @pl.when(i == 2)
    def _():
        def tile(t, carry):
            rows = pl.ds(t * TR, TR)
            out[0, rows, :] = (mm(n1[rows, :], weight()) + bias[0].astype(F32)).astype(BF)
            return carry

        lax.fori_loop(0, D // TR, tile, 0)

    @pl.when(i == 3)
    def _():
        def tile(t, carry):
            rows = pl.ds(t * TR, TR)
            out[0, rows, :] = mm_last(g[rows, :], weight()).astype(BF)
            return carry

        lax.fori_loop(0, D // TR, tile, 0)


def const2(shape):
    return pl.BlockSpec(shape, lambda i: (0,) * len(shape))


def smem():
    return pl.BlockSpec(memory_space=pltpu.SMEM)


def params():
    return pltpu.CompilerParams(
        dimension_semantics=("arbitrary",), vmem_limit_bytes=VMEM_LIMIT
    )


def cost(flops, bytes_accessed, transcendentals=0):
    return pl.CostEstimate(
        flops=flops, bytes_accessed=bytes_accessed, transcendentals=transcendentals
    )


PIECE = (8, 1, 32, D)
HALF = (16, 1, 32, D)


def pieces_at(place):
    return [pl.BlockSpec(PIECE, lambda i: (0, place(i), 0, 0))] * 4


def project(tab, n1, g, bias, tables, pieces_a, pieces_b):
    rows = n1.shape[0]
    return pl.pallas_call(
        project_kernel,
        grid=(4,),
        in_specs=[smem(), const2((rows, D)), const2((rows, D)),
                  pl.BlockSpec((1, 1, D), lambda i: (jnp.minimum(i, 2), 0, 0))]
        + [const2((rows, 128))] * 3 + pieces_at(lambda i: i // 3)
        + pieces_at(lambda i: i // 2),
        out_specs=pl.BlockSpec((1, rows, D), lambda i: (i, 0, 0)),
        out_shape=jax.ShapeDtypeStruct((4, rows, D), BF),
        scratch_shapes=[pltpu.VMEM((32, 32, D), BF)],
        compiler_params=params(),
        cost_estimate=cost(8 * rows * D * D, 20 * D * D),
        name="project",
    )(tab, n1, g, bias, *tables, *pieces_a, *pieces_b)


AQ = 256


def attention_kernel(segc, segr, cos, sa, sb, q, k, v, dm, *refs):
    mixed, dq, dk, dv, mask, dk_acc, dv_acc = refs[-7:]
    rows = q.shape[1]
    step = pl.program_id(0)

    @pl.when(step == 0)
    def _():
        for r in range(0, rows, AQ):
            n = r + AQ
            row_ids = r + lax.broadcasted_iota(jnp.int32, (AQ, n), 0)
            col_ids = lax.broadcasted_iota(jnp.int32, (AQ, n), 1)
            ok = (segc[r:r + AQ, :] == segr[:, :n]) & (col_ids <= row_ids)
            mask[r:r + AQ, :n] = jnp.where(ok, 0.0, MASKED)

    lane = lax.broadcasted_iota(jnp.int32, (1, 128), 1)
    dk_acc[...] = jnp.zeros_like(dk_acc)
    dv_acc[...] = jnp.zeros_like(dv_acc)
    zero = jnp.zeros((), BF)
    for r in range(0, rows, AQ):
        n = r + AQ
        blk = slice(r, r + AQ)
        mixed_sum = jnp.zeros((AQ, 128), F32)
        dq_sum = jnp.zeros((AQ, 128), F32)
        for h in range(2):
            own = (lane < 64) if h == 0 else (lane >= 64)
            kk, vv = k[0, :n, :], v[0, :n, :]
            qh = jnp.where(own, q[0, blk, :] * jnp.asarray(HD ** -0.5, BF), zero)
            dmh = jnp.where(own, dm[0, blk, :], zero)
            s = mm_last(qh, kk) + mask[blk, :n]
            top = jnp.max(s, axis=1, keepdims=True)
            e = jnp.exp(s - top)
            p = e * (1.0 / jnp.sum(e, axis=1, keepdims=True))
            pb = p.astype(BF)
            dp = mm_last(dmh, vv)
            delta = jnp.sum(p * dp, axis=1, keepdims=True)
            ds = (p * (dp - delta)).astype(BF)
            mixed_sum += mm(pb, jnp.where(own, vv, zero))
            dq_sum += mm(ds, jnp.where(own, kk, zero))
            dk_acc[:n, :] += mm_first(ds, qh)
            dv_acc[:n, :] += mm_first(pb, dmh)
        mixed[blk, :] = mixed_sum.astype(BF)
        dq[0, blk, :] = turn(
            dq_sum * HD ** -0.5, cos[blk, :], sa[blk, :], sb[blk, :], -1.0
        ).astype(BF)
    dk[0, :, :] = turn(dk_acc[...], cos[...], sa[...], sb[...], -1.0).astype(BF)
    dv[0, :, :] = dv_acc[...].astype(BF)


def attention(seg_col, seg_row, tables, qkvd, first, steps, earlier):
    rows = qkvd.shape[1]

    def part(p):
        return pl.BlockSpec((1, rows, 128), lambda i: (p, 0, i + first))

    def out3():
        return pl.BlockSpec((1, rows, 128), lambda i: (0, 0, i + first))

    return pl.pallas_call(
        attention_kernel,
        grid=(steps,),
        in_specs=[const2((rows, 1)), const2((1, rows))] + [const2((rows, 128))] * 3
        + [part(p) for p in range(4)] + [pl.BlockSpec(memory_space=pl.ANY)] * len(earlier),
        out_specs=[pl.BlockSpec((rows, 128), lambda i: (0, i + first))] + [out3()] * 3,
        out_shape=[jax.ShapeDtypeStruct((rows, D), BF)]
        + [jax.ShapeDtypeStruct((1, rows, D), BF)] * 3,
        scratch_shapes=[pltpu.VMEM((rows, rows), F32), pltpu.VMEM((rows, 128), F32),
                        pltpu.VMEM((rows, 128), F32)],
        input_output_aliases={9 + p: p for p in range(len(earlier))},
        compiler_params=params(),
        cost_estimate=cost(3 * steps * rows * rows * D, 2 * steps * rows * D,
                           2 * steps * rows * rows),
        name="attention",
    )(seg_col, seg_row, *tables, qkvd, qkvd, qkvd, qkvd, *earlier)


def weight_grad(left, right, keep, send, tab, base):
    def tile(t, carry):
        val = mm_first(left[:, pl.ds(t * TG, TG)], right)
        put_rows(keep, send, tab, base, tab[96], t, val)
        return carry

    lax.fori_loop(0, D // TG, tile, 0)


def input_grad(gj, weight, out, add):
    def tile(t, carry):
        rows = pl.ds(t * TR, TR)
        val = mm_last(gj[rows, :], weight())
        out[rows, :] = out[rows, :] + val if add else val
        return carry

    lax.fori_loop(0, gj.shape[0] // TR, tile, 0)


def dense_value_kernel(tab, n1, g, mixed, dv, *refs):
    pa, pb = refs[:4], refs[4:8]
    keep_a, send_a, keep_b, send_b, attn, gn1, bias, w_scr = refs[8:]

    def weight():
        return w_scr[...].reshape(D, D)

    @pl.when(pl.program_id(0) == 0)
    def _():
        assemble(w_scr, pa, tab, 0)

        def tile(t, carry):
            rows = pl.ds(t * TR, TR)
            attn[rows, :] = mm(mixed[rows, :], weight())
            return carry

        lax.fori_loop(0, mixed.shape[0] // TR, tile, 0)
        weight_grad(mixed, g[...], keep_a, send_a, tab, 64)

    @pl.when(pl.program_id(0) == 1)
    def _():
        assemble(w_scr, pb, tab, 32)
        bias[0, 0, :] = jnp.sum(dv[0].astype(F32), axis=0)
        input_grad(dv.at[0], weight, gn1, False)
        weight_grad(n1, dv[0], keep_b, send_b, tab, 80)


def query_key_kernel(tab, n1, dq, dk, *refs):
    pa, pb = refs[:4], refs[4:8]
    keep_a, send_a, keep_b, send_b, gn1, bias, w_scr = refs[8:]

    def weight():
        return w_scr[...].reshape(D, D)

    @pl.when(pl.program_id(0) == 0)
    def _():
        assemble(w_scr, pa, tab, 0)
        bias[0, 0, :] = jnp.sum(dq[0].astype(F32), axis=0)
        input_grad(dq.at[0], weight, gn1, False)
        weight_grad(n1, dq[0], keep_a, send_a, tab, 64)

    @pl.when(pl.program_id(0) == 1)
    def _():
        assemble(w_scr, pb, tab, 32)
        bias[1, 0, :] = jnp.sum(dk[0].astype(F32), axis=0)
        input_grad(dk.at[0], weight, gn1, True)
        weight_grad(n1, dk[0], keep_b, send_b, tab, 80)


def halves(blocks):
    return [jax.ShapeDtypeStruct((16, blocks, 32, D), BF)] * 4


def dense_value(tab, n1, g, mixed, dv, pieces_a, pieces_b):
    rows = n1.shape[0]
    full = jax.ShapeDtypeStruct((rows, D), F32)
    return pl.pallas_call(
        dense_value_kernel,
        grid=(2,),
        in_specs=[smem()] + [const2((rows, D))] * 3 + [const2((1, rows, D))]
        + pieces_at(lambda i: 1) + pieces_at(lambda i: 1),
        out_specs=[const2(HALF)] * 4 + [const2((rows, D))] * 2 + [const2((1, 1, D))],
        out_shape=halves(1) + [full, full, jax.ShapeDtypeStruct((1, 1, D), F32)],
        scratch_shapes=[pltpu.VMEM((32, 32, D), BF)],
        compiler_params=params(),
        cost_estimate=cost(8 * rows * D * D, 20 * D * D),
        name="dense_value",
    )(tab, n1, g, mixed, dv, *pieces_a, *pieces_b)


def query_key(tab, n1, dq, dk, pieces_a, pieces_b):
    rows = n1.shape[0]
    full = jax.ShapeDtypeStruct((rows, D), F32)
    return pl.pallas_call(
        query_key_kernel,
        grid=(2,),
        in_specs=[smem(), const2((rows, D))] + [const2((1, rows, D))] * 2
        + pieces_at(lambda i: 0) + pieces_at(lambda i: 0),
        out_specs=[const2(HALF)] * 4 + [const2((rows, D)), const2((2, 1, D))],
        out_shape=halves(1) + [full, jax.ShapeDtypeStruct((2, 1, D), F32)],
        scratch_shapes=[pltpu.VMEM((32, 32, D), BF)],
        compiler_params=params(),
        cost_estimate=cost(8 * rows * D * D, 20 * D * D),
        name="query_key",
    )(tab, n1, dq, dk, *pieces_a, *pieces_b)


def mlp_kernel(tab, n2, g, bias, *refs):
    pa, pb = refs[:4], refs[4:8]
    keep_a, send_a, keep_b, send_b, mlp, gn2, gbias = refs[-11:-4]
    w1_scr, w2_scr, act, gu = refs[-4:]
    mine = tab[96]
    assemble(w1_scr, pa, tab, 0)
    assemble(w2_scr, pb, tab, 32)

    @pl.when(pl.program_id(0) == 0)
    def _():
        mlp[...] = jnp.zeros_like(mlp)
        gn2[...] = jnp.zeros_like(gn2)

    def first():
        return w1_scr[...].reshape(D, D)

    def second():
        return w2_scr[...].reshape(D, D)

    gbias[...] = jnp.zeros_like(gbias)

    def tile(t, carry):
        rows = pl.ds(t * TR, TR)
        upper = mm(n2[rows, :], first()) + bias[0].astype(F32)
        cdf = 0.5 * (1.0 + lax.erf(upper * 2.0 ** -0.5))
        pdf = jnp.exp(-0.5 * upper * upper) * (2.0 * math.pi) ** -0.5
        active = (upper * cdf).astype(BF)
        act[rows, :] = active
        mlp[rows, :] += mm(active, second())
        grad = mm_last(g[rows, :], second()) * (cdf + upper * pdf)
        grad_b = grad.astype(BF)
        gu[rows, :] = grad_b
        gbias[0, 0, :] += jnp.sum(grad_b.astype(F32), axis=0)
        gn2[rows, :] += mm_last(grad_b, first())
        return carry

    lax.fori_loop(0, n2.shape[0] // TR, tile, 0)

    def grads(t, carry):
        cols = pl.ds(t * TG, TG)
        put_rows(keep_a, send_a, tab, 64, mine, t, mm_first(n2[:, cols], gu[...]))
        put_rows(keep_b, send_b, tab, 80, mine, t, mm_first(act[:, cols], g[...]))
        return carry

    lax.fori_loop(0, D // TG, grads, 0)


def mlp_part(tab, n2, g, bias, pieces_a, pieces_b, first, blocks, first_out, out_blocks, earlier):
    rows = n2.shape[0]
    vec_in = pl.BlockSpec((1, 1, D), lambda i: (i, 0, 0))
    vec_out = pl.BlockSpec((1, 1, D), lambda i: (i, 0, 0))
    half = pl.BlockSpec(HALF, lambda i: (0, i + first_out, 0, 0))
    full = jax.ShapeDtypeStruct((rows, D), F32)
    return pl.pallas_call(
        mlp_kernel,
        grid=(blocks,),
        in_specs=[smem(), const2((rows, D)), const2((rows, D)), vec_in]
        + pieces_at(lambda i: i + first) * 2
        + [pl.BlockSpec(memory_space=pl.ANY)] * len(earlier),
        out_specs=[half] * 4 + [const2((rows, D))] * 2 + [vec_out],
        out_shape=halves(out_blocks)
        + [full, full, jax.ShapeDtypeStruct((blocks, 1, D), F32)],
        scratch_shapes=[pltpu.VMEM((32, 32, D), BF)] * 2 + [pltpu.VMEM((rows, D), BF)] * 2,
        input_output_aliases={12 + p: p for p in range(len(earlier))},
        compiler_params=params(),
        cost_estimate=cost(12 * blocks * rows * D * D, 14 * blocks * D * D, 2 * blocks * rows * D),
        name="mlp",
    )(tab, n2, g, bias, *pieces_a, *pieces_b, *earlier)


def locate(lengths, device_of, offsets, rows, which):
    row_ids = jnp.arange(rows, dtype=jnp.int32)
    inside = (
        (device_of[None, :] == which)
        & (row_ids[:, None] >= offsets[None, :])
        & (row_ids[:, None] < offsets[None, :] + lengths[None, :])
    ).astype(jnp.int32)
    found_any = jnp.sum(inside, axis=1)
    numbers = jnp.arange(lengths.shape[0], dtype=jnp.int32)
    segment = jnp.where(
        found_any > 0, jnp.sum(inside * numbers[None, :], axis=1), lengths.shape[0] + row_ids
    )
    position = jnp.where(found_any > 0, row_ids - jnp.sum(inside * offsets[None, :], axis=1), 0)
    return (segment, position)


def rotary_tables(position):
    lane = jnp.arange(128, dtype=jnp.int32)[None, :] % HD
    half_rot = ROT // 2
    exponent = (lane % half_rot).astype(F32) * (2.0 / ROT)
    angles = position.astype(F32)[:, None] * jnp.exp(-math.log(10000.0) * exponent)
    cosine, sine = jnp.cos(angles), jnp.sin(angles)
    return (
        jnp.where(lane < ROT, cosine, 1.0),
        jnp.where(lane < half_rot, sine, 0.0),
        jnp.where((lane >= half_rot) & (lane < ROT), sine, 0.0),
    )


def after(value, *others):
    return lax.optimization_barrier((value, others))[0]


class Chips:
    size = 32
    core = [(i, i ^ 1) for i in range(32)]
    x_way = [(i, i ^ 2) for i in range(32)]
    y_way = [(i, i ^ 4) for i in range(32)]
    z_ways = [[(i, (i + 8 * s) % 32) for i in range(32)] for s in range(4)]

    @staticmethod
    def table(me):
        z, y, x, c = me // 8, (me // 4) % 2, (me // 2) % 2, me % 2
        k = jnp.arange(32, dtype=jnp.int32)
        piece_c, piece_hi, mid, zr = k // 16, (k // 8) % 2, (k // 4) % 2, k % 4
        zz, cc = (z - zr) % 4, c ^ piece_c
        from_a = ((zz * 2 + (y ^ mid)) * 2 + (x ^ piece_hi)) * 2 + cc
        from_b = ((zz * 2 + (y ^ piece_hi)) * 2 + (x ^ mid)) * 2 + cc
        j = jnp.arange(16, dtype=jnp.int32)
        jz, jy, jx = (j // 4 - z) % 4, ((j // 2) % 2) ^ y, (j % 2) ^ x
        to_a = jx * 8 + jy * 4 + jz
        to_b = jy * 8 + jx * 4 + jz
        return jnp.concatenate([from_a, from_b, to_a, to_b, c[None]]).astype(jnp.int32)


def send(value, way):
    return lax.ppermute(value, "fsdp", way)


def beside(value, way, kernel):
    return after(send(value, way), kernel[-1])


def gather_z(shards):
    return [shards] + [send(shards, Chips.z_ways[s]) for s in (1, 2, 3)]


def stack_z(by_z, lo, hi):
    return jnp.stack([v[lo:hi] for v in by_z], axis=0)


def scatter_one(keep, got):
    total = lambda lo, hi: keep[lo:hi].astype(F32) + got[lo:hi].astype(F32)
    away = total(8, 16).astype(BF)
    return away, total


def scatter_two(total, got):
    more = lambda lo, hi: total(lo, hi) + got[lo:hi].astype(F32)
    return more(4, 8).astype(BF), more


def scatter_z(more_a, got_a, more_b, got_b):
    def at(s):
        a = more_a(s, s + 1)[0] + got_a[s].astype(F32)
        b = more_b(s, s + 1)[0] + got_b[s].astype(F32)
        return jnp.concatenate([a, b], axis=0)

    return at


def keep_whole(keep_a, send_a, keep_b, send_b):
    def one(keep, other):
        pairs = jnp.stack([keep, other], axis=1).transpose(2, 0, 1, 3, 4)
        return pairs.reshape(keep.shape[1], D, D).astype(F32)

    return one(keep_a, send_a), one(keep_b, send_b)


def gather_any(blocks):
    whole = lax.all_gather(blocks, "fsdp", axis=1, tiled=True)
    return in_pieces(whole.reshape(blocks.shape[0], 32, 32, D))


def in_pieces(whole):
    whole = whole.transpose(1, 0, 2, 3)
    return tuple(whole[8 * p : 8 * p + 8] for p in range(4))


def on_device(
    devices,
    tokens,
    out_cotangent,
    seq_lengths,
    seq_device,
    seq_offset,
    ln1_gain,
    ln1_bias,
    qkv_weight,
    qkv_bias,
    dense_weight,
    dense_bias,
    ln2_gain,
    ln2_bias,
    fc1_weight,
    fc1_bias,
    fc2_weight,
    fc2_bias,
):
    rows = tokens.shape[0]
    which = lax.axis_index("fsdp")
    chips = devices == Chips.size
    own_d = D // devices
    core, x_way, y_way, z_ways = Chips.core, Chips.x_way, Chips.y_way, Chips.z_ways

    vectors = (ln1_gain, ln1_bias, dense_bias, ln2_gain, ln2_bias, fc2_bias, qkv_bias, fc1_bias)
    packed = jnp.concatenate(vectors)
    packed = jnp.pad(packed, (0, -packed.shape[0] % 1024)).reshape(-1, 128)
    q_w, k_w, v_w = [qkv_weight[:, p * D : p * D + D] for p in range(3)]
    if chips:
        tab = Chips.table(which)
        fc1_shard = (
            fc1_weight.reshape(32, 32, 4, 32).transpose(2, 0, 1, 3).reshape(4, 32, D)
        )
        fc2_shard = fc2_weight.reshape(4, 32, D)
        z0 = gather_z(jnp.concatenate([fc1_shard[:2], fc2_shard[:2]], axis=0))
        z1 = gather_z(after(jnp.concatenate([fc1_shard[2:], fc2_shard[2:]], axis=0), *z0))
        vec4 = jnp.concatenate([v[None] for v in gather_z(after(packed, *z0))], axis=0)
        za, zb = stack_z(z0, 0, 2), stack_z(z0, 2, 4)
        near_a = jnp.concatenate([za, send(za, y_way)], axis=0)
        near_b = jnp.concatenate([zb, send(zb, x_way)], axis=0)
        vec8 = jnp.concatenate([vec4, send(vec4, y_way)], axis=0)
        far_a, far_b = send(near_a, x_way), send(near_b, y_way)
        vec16 = jnp.concatenate([vec8, send(vec8, x_way)], axis=0)
        m0_a = (near_a, far_a, send(near_a, core), send(far_a, core))
        m0_b = (near_b, far_b, send(near_b, core), send(far_b, core))
        vec32 = jnp.concatenate([vec16, send(vec16, core)], axis=0)
        places = jnp.arange(32, dtype=jnp.int32)
        pick = (tab[None, :32] == places[:, None]).astype(BF)
        packed = mm(pick, vec32.reshape(32, -1))
    else:
        ident = jnp.arange(32, dtype=jnp.int32)
        tab = jnp.concatenate([ident, ident, ident[:16], ident[:16], ident[:1]])
        packed = lax.all_gather(packed, "fsdp", axis=0, tiled=True).reshape(devices, -1)
        packed = packed.astype(F32)
        fc1 = gather_any(fc1_weight.reshape(own_d, 4, D).transpose(1, 0, 2))
        fc2 = lax.all_gather(fc2_weight, "fsdp", axis=0, tiled=True)
        fc2 = in_pieces(fc2.reshape(4, 32, 32, D))
        m0_a, m1_a = tuple(w[:, :2] for w in fc1), tuple(w[:, 2:] for w in fc1)
        m0_b, m1_b = tuple(w[:, :2] for w in fc2), tuple(w[:, 2:] for w in fc2)
        t_a = gather_any(jnp.stack([q_w, dense_weight]))
        t_b = gather_any(jnp.stack([k_w, v_w]))

    full, at = [], 0
    for v in vectors:
        full.append(packed[:, at : at + v.shape[0]])
        at += v.shape[0]
    gain1, bias1, dense_b, gain2, bias2, fc2_b, qkv_b = [v.reshape(-1) for v in full[:7]]
    qkv_b = qkv_b.reshape(3, 1, D)
    if chips:
        fc1_b = full[7].reshape(32, 4, 32).transpose(1, 0, 2).reshape(4, 1, D)
    else:
        fc1_b = full[7].reshape(4, 1, D)

    segment, position = locate(seq_lengths, seq_device, seq_offset, rows, which)
    tables = rotary_tables(position)
    rows_in = tokens.astype(F32)
    row_mean = jnp.mean(rows_in, axis=-1, keepdims=True)
    centred = rows_in - row_mean
    row_var = jnp.mean(centred * centred, axis=-1, keepdims=True)
    scale = lax.rsqrt(row_var + EPSILON)
    normal = centred * scale
    n1 = (normal * gain1 + bias1).astype(BF)
    n2 = (normal * gain2 + bias2).astype(BF)
    grad_out = out_cotangent.astype(F32)
    cotangent_sum = jnp.sum(grad_out, axis=0)
    g = out_cotangent
    seg_col, seg_row = segment[:, None], segment[None, :]

    def mlp(data, block, pieces, earlier):
        return mlp_part(
            tab, data, g, fc1_b[block : block + 1], *pieces, block % 2, 1, block % 2, 2, earlier
        )

    if chips:
        za, zb = after((stack_z(z1, 0, 2), stack_z(z1, 2, 4)), far_a, far_b)
        t_shards = after(jnp.stack([q_w, dense_weight, k_w, v_w]), far_a, far_b)
        r0 = mlp(after(n2, za, zb, t_shards, n1, tables, seg_col, seg_row, qkv_b), 0, (m0_a, m0_b), ())
        near_a = jnp.concatenate([za, beside(za, y_way, r0)], axis=0)
        near_b = jnp.concatenate([zb, beside(zb, x_way, r0)], axis=0)
        zt = gather_z(t_shards)
        zt = [zt[0], *after(zt[1:], r0[4])]
        r1 = mlp(after(n2, near_a, near_b, r0[4]), 1, (m0_a, m0_b), r0[:4])
        far_a, far_b = beside(near_a, x_way, r1), beside(near_b, y_way, r1)
        m1_a = (near_a, far_a, send(near_a, core), send(far_a, core))
        m1_b = (near_b, far_b, send(near_b, core), send(far_b, core))
        za, zb = after((stack_z(zt, 0, 2), stack_z(zt, 2, 4)), far_a, far_b)
        r2 = mlp(after(n2, za, zb, r1[4]), 2, (m1_a, m1_b), ())
        near_a = jnp.concatenate([za, beside(za, y_way, r2)], axis=0)
        near_b = jnp.concatenate([zb, beside(zb, x_way, r2)], axis=0)
        got_a, got_b = beside(r1[1], core, r2), beside(r1[3], core, r2)
        r3 = mlp(after(n2, near_a, near_b, got_a, got_b, r2[4]), 3, (m1_a, m1_b), r2[:4])
        far_a, far_b = beside(near_a, x_way, r3), beside(near_b, y_way, r3)
        t_a = (near_a, far_a, send(near_a, core), send(far_a, core))
        t_b = (near_b, far_b, send(near_b, core), send(far_b, core))
        keep = after((r1[0], r1[2]), r3[4])
        away_a, sum_a = scatter_one(keep[0], got_a)
        away_b, sum_b = scatter_one(keep[1], got_b)
        qkvd = project(tab, after(n1, away_a, away_b, r3[4]), g, qkv_b, tables, t_a, t_b)
        got_a, got_b = beside(away_a, x_way, [qkvd]), beside(away_b, y_way, [qkvd])
        far2_a, far2_b = beside(r3[1], core, [qkvd]), beside(r3[3], core, [qkvd])
        away_a, more_a = scatter_two(sum_a, got_a)
        away_b, more_b = scatter_two(sum_b, got_b)
        away2_a, sum2_a = scatter_one(r3[0], far2_a)
        away2_b, sum2_b = scatter_one(r3[2], far2_b)
        first = attention(
            seg_col, seg_row, tables, after(qkvd, away_a, away_b, away2_a, away2_b), 0, 4, ()
        )
        got_a, got_b = beside(away_a, y_way, first), beside(away_b, x_way, first)
        got2_a, got2_b = beside(away2_a, x_way, first), beside(away2_b, y_way, first)
        z_part = scatter_z(more_a, got_a, more_b, got_b)
        z_away = [z_part(s).astype(BF) for s in (1, 2, 3)]
        away2_a, more2_a = scatter_two(sum2_a, got2_a)
        away2_b, more2_b = scatter_two(sum2_b, got2_b)
        second = attention(
            seg_col, seg_row, tables, after(qkvd, z_away, away2_a, away2_b), 4, 4, first
        )
        mixed, dq, dk, dv = second
        z_got = [beside(v, z_ways[s + 1], second) for s, v in enumerate(z_away)]
        got2_a, got2_b = beside(away2_a, y_way, second), beside(away2_b, x_way, second)
        z_part2 = scatter_z(more2_a, got2_a, more2_b, got2_b)
        z_away2 = [z_part2(s).astype(BF) for s in (1, 2, 3)]
        b1 = dense_value(tab, after(n1, z_away2, z_got), g, mixed, dv, t_a, t_b)
        z_got2 = [beside(v, z_ways[s + 1], b1) for s, v in enumerate(z_away2)]
        got_a, got_b = send(b1[1], core), send(b1[3], core)
        away_a, sum_a = scatter_one(b1[0], got_a)
        away_b, sum_b = scatter_one(b1[2], got_b)
        b2 = query_key(tab, after(n1, away_a, away_b), dq, dk, t_a, t_b)
        got_a, got_b = beside(away_a, x_way, b2), beside(away_b, y_way, b2)
        got2_a, got2_b = send(b2[1], core), send(b2[3], core)
        away2_a, sum2_a = scatter_one(b2[0], got2_a)
        away2_b, sum2_b = scatter_one(b2[2], got2_b)
        late_0, late_1, *late = after(
            [z_part(0), z_part2(0), b1[4], b1[5], b2[4]] + [r[p] for r in (r0, r1, r2, r3) for p in (4, 5)],
            away2_a, away2_b,
        )
        own0 = late_0 + sum(v.astype(F32) for v in z_got)
        own1 = late_1 + sum(v.astype(F32) for v in z_got2)
    else:
        r0 = mlp(n2, 0, (m0_a, m0_b), ())
        r1 = mlp(n2, 1, (m0_a, m0_b), r0[:4])
        r2 = mlp(n2, 2, (m1_a, m1_b), ())
        r3 = mlp(n2, 3, (m1_a, m1_b), r2[:4])
        qkvd = project(tab, n1, g, qkv_b, tables, t_a, t_b)
        first = attention(seg_col, seg_row, tables, qkvd, 0, 4, ())
        mixed, dq, dk, dv = attention(seg_col, seg_row, tables, qkvd, 4, 4, first)
        b1 = dense_value(tab, n1, g, mixed, dv, t_a, t_b)
        b2 = query_key(tab, n1, dq, dk, t_a, t_b)
        late = [b1[4], b1[5], b2[4]] + [r[p] for r in (r0, r1, r2, r3) for p in (4, 5)]

    attn_out, gn1 = late[0], late[1] + late[2]
    mlp_out = late[3] + late[5] + late[7] + late[9]
    gn2 = late[4] + late[6] + late[8] + late[10]
    grad_ln1_g = jnp.sum(gn1 * normal, axis=0)
    grad_ln1_b = jnp.sum(gn1, axis=0)
    grad_ln2_g = jnp.sum(gn2 * normal, axis=0)
    grad_ln2_b = jnp.sum(gn2, axis=0)
    gqkv_b = jnp.concatenate([b2[5], b1[6]], axis=0)
    gfc1_b = jnp.concatenate([r0[6], r1[6], r2[6], r3[6]], axis=0)[:, 0]
    if chips:
        gfc1_b = gfc1_b.reshape(4, 32, 32).transpose(1, 0, 2)
    small = [
        v.reshape(devices, -1)
        for v in (grad_ln1_g, grad_ln1_b, cotangent_sum, grad_ln2_g, grad_ln2_b, gqkv_b, gfc1_b)
    ]
    joint = jnp.concatenate(small, axis=1)
    if chips:
        j = places // 2
        slot = ((places % 2) ^ (which % 2)) * 16 + jnp.take(tab[64:80], j)
        to_slot = (slot[None, :] == places[:, None]).astype(F32)
        joint = jnp.dot(to_slot, joint, precision=lax.Precision.HIGHEST)
        joint = joint[:16] + send(joint[16:], core)
        joint = joint[:8] + send(joint[8:], x_way)
        joint = joint[:4] + send(joint[4:], y_way)
        owned = joint[0] + sum(send(joint[s], z_ways[s]) for s in (1, 2, 3))
    else:
        joint = jnp.pad(joint, ((0, 0), (0, -joint.shape[1] % 1024))).reshape(-1, 128)
        owned = lax.psum_scatter(joint, "fsdp", scatter_dimension=0, tiled=True).reshape(-1)
    out, at = [], 0
    for v in small:
        out.append(owned[at : at + v.shape[1]])
        at += v.shape[1]
    o_ln1_g, o_ln1_b, o_cot, o_ln2_g, o_ln2_b, o_qkv_b, o_fc1_b = out

    if chips:
        got2_a, got2_b = send(b2[1], core), send(b2[3], core)
        away2_a, sum2_a = scatter_one(b2[0], got2_a)
        away2_b, sum2_b = scatter_one(b2[2], got2_b)
        got_a, got_b = send(away_a, x_way), send(away_b, y_way)
        away_a, more_a = scatter_two(sum_a, got_a)
        away_b, more_b = scatter_two(sum_b, got_b)
        got2_a, got2_b = send(away2_a, x_way), send(away2_b, y_way)
        got_a, got_b = send(away_a, y_way), send(away_b, x_way)
        z_part = scatter_z(more_a, got_a, more_b, got_b)
        away2_a, more2_a = scatter_two(sum2_a, got2_a)
        away2_b, more2_b = scatter_two(sum2_b, got2_b)
        got2_a, got2_b = send(away2_a, y_way), send(away2_b, x_way)
        z_part2 = scatter_z(more2_a, got2_a, more2_b, got2_b)
        z_sum = lambda part: part(0) + sum(
            send(part(s).astype(BF), z_ways[s]).astype(F32) for s in (1, 2, 3)
        )
        own_b1, own_b2 = z_sum(z_part), z_sum(z_part2)
        g_fc1 = jnp.concatenate([own0[:2], own1[:2]], axis=0)
        g_fc2 = jnp.concatenate([own0[2:], own1[2:]], axis=0)
        g_fc1 = g_fc1.reshape(4, 32, 32, 32).transpose(1, 2, 0, 3).reshape(32, FF)
        g_fc2 = g_fc2.reshape(128, D)
        g_t = (own_b2[0], own_b2[1], own_b1[1], own_b1[0])
    else:
        first, second = keep_whole(*r1[:4]), keep_whole(*r3[:4])
        g_fc1 = jnp.concatenate([first[0], second[0]], axis=0)
        g_fc2 = jnp.concatenate([first[1], second[1]], axis=0)
        g_fc1 = lax.psum_scatter(g_fc1, "fsdp", scatter_dimension=1, tiled=True)
        g_fc1 = g_fc1.transpose(1, 0, 2).reshape(own_d, FF)
        g_fc2 = lax.psum_scatter(
            g_fc2.reshape(FF, D), "fsdp", scatter_dimension=0, tiled=True
        )
        dense_part, value_part = keep_whole(*b1[:4])
        g_t = lax.psum_scatter(
            jnp.concatenate([*keep_whole(*b2[:4]), value_part, dense_part], axis=0),
            "fsdp", scatter_dimension=1, tiled=True,
        )
    g_qkv = jnp.concatenate(g_t[:3], axis=1)
    g_dense = g_t[3]

    result = (
        rows_in + attn_out + dense_b + mlp_out + fc2_b
    ).astype(BF)
    into = gn1 * gain1 + gn2 * gain2
    back = scale * (
        into
        - jnp.mean(into, axis=-1, keepdims=True)
        - normal * jnp.mean(into * normal, axis=-1, keepdims=True)
    )
    grad_tokens = (grad_out + back).astype(BF)
    return (
        result, grad_tokens, o_ln1_g, o_ln1_b, g_qkv, o_qkv_b, g_dense, o_cot,
        o_ln2_g, o_ln2_b, g_fc1, o_fc1_b, g_fc2, o_cot,
    )


def solution(mesh):
    rows, vec, whole = P("fsdp", None), P("fsdp"), P()
    return jax.shard_map(
        partial(on_device, mesh.shape["fsdp"]),
        mesh=mesh,
        in_specs=(
            rows, rows, whole, whole, whole, vec, vec, rows, vec, rows, vec, vec, vec,
            rows, vec, rows, vec,
        ),
        out_specs=(
            rows, rows, vec, vec, rows, vec, rows, vec, vec, vec, rows, vec, rows, vec,
        ),
        check_vma=False,
    )
```

```python
from functools import partial
import math

import jax
import jax.numpy as jnp
from jax import lax
from jax.experimental import pallas as pl
from jax.experimental.pallas import tpu as pltpu
from jax.sharding import PartitionSpec as P

D = 1024
H = 16
HD = 64
ROT = 16
FF = 4096

EPSILON = 1e-05
MASKED = -1e30
BF = jnp.bfloat16
F32 = jnp.float32
LAST = (((1,), (1,)), ((), ()))
FIRST = (((0,), (0,)), ((), ()))
VMEM_LIMIT = 60 * 1024 * 1024


def mm(a, b):
    return jnp.dot(a, b, preferred_element_type=F32)


def mm_last(a, b):
    return lax.dot_general(a, b, LAST, preferred_element_type=F32)


def mm_first(a, b):
    return lax.dot_general(a, b, FIRST, preferred_element_type=F32)


def assemble(w_scr, pieces, tab, base):
    for p, piece in enumerate(pieces):
        for j in range(8):
            w_scr[tab[base + p * 8 + j]] = piece[j, 0]


def put_rows(keep_ref, send_ref, tab, base, mine, tile, values):
    pairs = values.shape[0] // 64
    blocks = values.astype(BF).reshape(pairs, 2, 32, values.shape[1])
    even, odd = blocks[:, 0], blocks[:, 1]
    keep = jnp.where(mine == 0, even, odd)
    send = jnp.where(mine == 0, odd, even)
    for j in range(pairs):
        slot = tab[base + tile * pairs + j]
        keep_ref[slot, 0] = keep[j]
        send_ref[slot, 0] = send[j]


def turn(x, cosine, sine_a, sine_b, sign):
    left = pltpu.roll(x, x.shape[1] - ROT // 2, 1)
    right = pltpu.roll(x, ROT // 2, 1)
    return x * cosine - sign * (left * sine_a - right * sine_b)


TR = 1024
TG = 1024


def project_kernel(tab, n1, g, bias, cos, sa, sb, *refs):
    pa, pb, out, w_scr = refs[:4], refs[4:8], refs[8], refs[9]
    i = pl.program_id(0)
    from_b = (i == 1) | (i == 2)

    @pl.when(jnp.logical_not(from_b))
    def _():
        assemble(w_scr, pa, tab, 0)

    @pl.when(from_b)
    def _():
        assemble(w_scr, pb, tab, 32)

    def weight():
        return w_scr[...].reshape(D, D)

    @pl.when(i < 2)
    def _():
        def tile(t, carry):
            rows = pl.ds(t * TR, TR)
            val = mm(n1[rows, :], weight()) + bias[0].astype(F32)
            c, a, b = cos[rows, :], sa[rows, :], sb[rows, :]
            for j in range(D // 128):
                cols = slice(j * 128, j * 128 + 128)
                out[0, rows, cols] = turn(val[:, cols], c, a, b, 1.0).astype(BF)
            return carry

        lax.fori_loop(0, D // TR, tile, 0)

    @pl.when(i == 2)
    def _():
        def tile(t, carry):
            rows = pl.ds(t * TR, TR)
            out[0, rows, :] = (mm(n1[rows, :], weight()) + bias[0].astype(F32)).astype(BF)
            return carry

        lax.fori_loop(0, D // TR, tile, 0)

    @pl.when(i == 3)
    def _():
        def tile(t, carry):
            rows = pl.ds(t * TR, TR)
            out[0, rows, :] = mm_last(g[rows, :], weight()).astype(BF)
            return carry

        lax.fori_loop(0, D // TR, tile, 0)


def const2(shape):
    return pl.BlockSpec(shape, lambda i: (0,) * len(shape))


def smem():
    return pl.BlockSpec(memory_space=pltpu.SMEM)


def params():
    return pltpu.CompilerParams(
        dimension_semantics=("arbitrary",), vmem_limit_bytes=VMEM_LIMIT
    )


def cost(flops, bytes_accessed, transcendentals=0):
    return pl.CostEstimate(
        flops=flops, bytes_accessed=bytes_accessed, transcendentals=transcendentals
    )


PIECE = (8, 1, 32, D)
HALF = (16, 1, 32, D)


def pieces_at(place):
    return [pl.BlockSpec(PIECE, lambda i: (0, place(i), 0, 0))] * 4


def project(tab, n1, g, bias, tables, pieces_a, pieces_b):
    rows = n1.shape[0]
    return pl.pallas_call(
        project_kernel,
        grid=(4,),
        in_specs=[smem(), const2((rows, D)), const2((rows, D)),
                  pl.BlockSpec((1, 1, D), lambda i: (jnp.minimum(i, 2), 0, 0))]
        + [const2((rows, 128))] * 3 + pieces_at(lambda i: i // 3)
        + pieces_at(lambda i: i // 2),
        out_specs=pl.BlockSpec((1, rows, D), lambda i: (i, 0, 0)),
        out_shape=jax.ShapeDtypeStruct((4, rows, D), BF),
        scratch_shapes=[pltpu.VMEM((32, 32, D), BF)],
        compiler_params=params(),
        cost_estimate=cost(8 * rows * D * D, 20 * D * D),
        name="project",
    )(tab, n1, g, bias, *tables, *pieces_a, *pieces_b)


AQ = 256


def attention_kernel(segc, segr, cos, sa, sb, q, k, v, dm, *refs):
    mixed, dq, dk, dv, mask, dk_acc, dv_acc = refs[-7:]
    rows = q.shape[1]
    step = pl.program_id(0)

    @pl.when(step == 0)
    def _():
        for r in range(0, rows, AQ):
            n = r + AQ
            row_ids = r + lax.broadcasted_iota(jnp.int32, (AQ, n), 0)
            col_ids = lax.broadcasted_iota(jnp.int32, (AQ, n), 1)
            ok = (segc[r:r + AQ, :] == segr[:, :n]) & (col_ids <= row_ids)
            mask[r:r + AQ, :n] = jnp.where(ok, 0.0, MASKED)

    lane = lax.broadcasted_iota(jnp.int32, (1, 128), 1)
    dk_acc[...] = jnp.zeros_like(dk_acc)
    dv_acc[...] = jnp.zeros_like(dv_acc)
    zero = jnp.zeros((), BF)
    for r in range(0, rows, AQ):
        n = r + AQ
        blk = slice(r, r + AQ)
        mixed_sum = jnp.zeros((AQ, 128), F32)
        dq_sum = jnp.zeros((AQ, 128), F32)
        for h in range(2):
            own = (lane < 64) if h == 0 else (lane >= 64)
            kk, vv = k[0, :n, :], v[0, :n, :]
            qh = jnp.where(own, q[0, blk, :] * jnp.asarray(HD ** -0.5, BF), zero)
            dmh = jnp.where(own, dm[0, blk, :], zero)
            s = mm_last(qh, kk) + mask[blk, :n]
            top = jnp.max(s, axis=1, keepdims=True)
            e = jnp.exp(s - top)
            p = e * (1.0 / jnp.sum(e, axis=1, keepdims=True))
            pb = p.astype(BF)
            dp = mm_last(dmh, vv)
            delta = jnp.sum(p * dp, axis=1, keepdims=True)
            ds = (p * (dp - delta)).astype(BF)
            mixed_sum += mm(pb, jnp.where(own, vv, zero))
            dq_sum += mm(ds, jnp.where(own, kk, zero))
            dk_acc[:n, :] += mm_first(ds, qh)
            dv_acc[:n, :] += mm_first(pb, dmh)
        mixed[blk, :] = mixed_sum.astype(BF)
        dq[0, blk, :] = turn(
            dq_sum * HD ** -0.5, cos[blk, :], sa[blk, :], sb[blk, :], -1.0
        ).astype(BF)
    dk[0, :, :] = turn(dk_acc[...], cos[...], sa[...], sb[...], -1.0).astype(BF)
    dv[0, :, :] = dv_acc[...].astype(BF)


def attention(seg_col, seg_row, tables, qkvd, first, steps, earlier):
    rows = qkvd.shape[1]

    def part(p):
        return pl.BlockSpec((1, rows, 128), lambda i: (p, 0, i + first))

    def out3():
        return pl.BlockSpec((1, rows, 128), lambda i: (0, 0, i + first))

    return pl.pallas_call(
        attention_kernel,
        grid=(steps,),
        in_specs=[const2((rows, 1)), const2((1, rows))] + [const2((rows, 128))] * 3
        + [part(p) for p in range(4)] + [pl.BlockSpec(memory_space=pl.ANY)] * len(earlier),
        out_specs=[pl.BlockSpec((rows, 128), lambda i: (0, i + first))] + [out3()] * 3,
        out_shape=[jax.ShapeDtypeStruct((rows, D), BF)]
        + [jax.ShapeDtypeStruct((1, rows, D), BF)] * 3,
        scratch_shapes=[pltpu.VMEM((rows, rows), F32), pltpu.VMEM((rows, 128), F32),
                        pltpu.VMEM((rows, 128), F32)],
        input_output_aliases={9 + p: p for p in range(len(earlier))},
        compiler_params=params(),
        cost_estimate=cost(3 * steps * rows * rows * D, 2 * steps * rows * D,
                           2 * steps * rows * rows),
        name="attention",
    )(seg_col, seg_row, *tables, qkvd, qkvd, qkvd, qkvd, *earlier)


def weight_grad(left, right, keep, send, tab, base):
    def tile(t, carry):
        val = mm_first(left[:, pl.ds(t * TG, TG)], right)
        put_rows(keep, send, tab, base, tab[96], t, val)
        return carry

    lax.fori_loop(0, D // TG, tile, 0)


def input_grad(gj, weight, out, add=None):
    def tile(t, carry):
        rows = pl.ds(t * TR, TR)
        val = mm_last(gj[rows, :], weight())
        val = val if add is None else add[rows, :] + val
        out[rows, :] = val.astype(out.dtype)
        return carry

    lax.fori_loop(0, gj.shape[0] // TR, tile, 0)


def dense_value_kernel(tab, n1, g, mixed, dv, *refs):
    pa, pb = refs[:4], refs[4:8]
    keep_a, send_a, keep_b, send_b, attn, gn1, bias, w_scr = refs[8:]

    def weight():
        return w_scr[...].reshape(D, D)

    @pl.when(pl.program_id(0) == 0)
    def _():
        assemble(w_scr, pa, tab, 0)

        def tile(t, carry):
            rows = pl.ds(t * TR, TR)
            attn[rows, :] = mm(mixed[rows, :], weight()).astype(BF)
            return carry

        lax.fori_loop(0, mixed.shape[0] // TR, tile, 0)
        weight_grad(mixed, g[...], keep_a, send_a, tab, 64)

    @pl.when(pl.program_id(0) == 1)
    def _():
        assemble(w_scr, pb, tab, 32)
        bias[0, 0, :] = jnp.sum(dv[0].astype(F32), axis=0)
        input_grad(dv.at[0], weight, gn1)
        weight_grad(n1, dv[0], keep_b, send_b, tab, 80)


def query_key_kernel(tab, n1, dq, dk, *refs):
    pa, pb = refs[:4], refs[4:8]
    keep_a, send_a, keep_b, send_b, gn1, bias, w_scr, gn1_scr = refs[8:]

    def weight():
        return w_scr[...].reshape(D, D)

    @pl.when(pl.program_id(0) == 0)
    def _():
        assemble(w_scr, pa, tab, 0)
        bias[0, 0, :] = jnp.sum(dq[0].astype(F32), axis=0)
        input_grad(dq.at[0], weight, gn1_scr)
        weight_grad(n1, dq[0], keep_a, send_a, tab, 64)

    @pl.when(pl.program_id(0) == 1)
    def _():
        assemble(w_scr, pb, tab, 32)
        bias[1, 0, :] = jnp.sum(dk[0].astype(F32), axis=0)
        input_grad(dk.at[0], weight, gn1, gn1_scr)
        weight_grad(n1, dk[0], keep_b, send_b, tab, 80)


def halves(blocks):
    return [jax.ShapeDtypeStruct((16, blocks, 32, D), BF)] * 4


def dense_value(tab, n1, g, mixed, dv, pieces_a, pieces_b):
    rows = n1.shape[0]
    full = jax.ShapeDtypeStruct((rows, D), BF)
    return pl.pallas_call(
        dense_value_kernel,
        grid=(2,),
        in_specs=[smem()] + [const2((rows, D))] * 3 + [const2((1, rows, D))]
        + pieces_at(lambda i: 1) + pieces_at(lambda i: 1),
        out_specs=[const2(HALF)] * 4 + [const2((rows, D))] * 2 + [const2((1, 1, D))],
        out_shape=halves(1) + [full, full, jax.ShapeDtypeStruct((1, 1, D), F32)],
        scratch_shapes=[pltpu.VMEM((32, 32, D), BF)],
        compiler_params=params(),
        cost_estimate=cost(8 * rows * D * D, 20 * D * D),
        name="dense_value",
    )(tab, n1, g, mixed, dv, *pieces_a, *pieces_b)


def query_key(tab, n1, dq, dk, pieces_a, pieces_b):
    rows = n1.shape[0]
    full = jax.ShapeDtypeStruct((rows, D), BF)
    return pl.pallas_call(
        query_key_kernel,
        grid=(2,),
        in_specs=[smem(), const2((rows, D))] + [const2((1, rows, D))] * 2
        + pieces_at(lambda i: 0) + pieces_at(lambda i: 0),
        out_specs=[const2(HALF)] * 4 + [const2((rows, D)), const2((2, 1, D))],
        out_shape=halves(1) + [full, jax.ShapeDtypeStruct((2, 1, D), F32)],
        scratch_shapes=[pltpu.VMEM((32, 32, D), BF), pltpu.VMEM((rows, D), F32)],
        compiler_params=params(),
        cost_estimate=cost(8 * rows * D * D, 20 * D * D),
        name="query_key",
    )(tab, n1, dq, dk, *pieces_a, *pieces_b)


def mlp_kernel(tab, n2, g, bias, *refs):
    pa, pb = refs[:4], refs[4:8]
    keep_a, send_a, keep_b, send_b, mlp, gn2, gbias = refs[-11:-4]
    w1_scr, w2_scr, act, gu = refs[-4:]
    mine = tab[96]
    assemble(w1_scr, pa, tab, 0)
    assemble(w2_scr, pb, tab, 32)

    def first():
        return w1_scr[...].reshape(D, D)

    def second():
        return w2_scr[...].reshape(D, D)

    gbias[...] = jnp.zeros_like(gbias)

    def tile(t, carry):
        rows = pl.ds(t * TR, TR)
        upper = mm(n2[rows, :], first()) + bias[0].astype(F32)
        cdf = 0.5 * (1.0 + lax.erf(upper * 2.0 ** -0.5))
        pdf = jnp.exp(-0.5 * upper * upper) * (2.0 * math.pi) ** -0.5
        active = (upper * cdf).astype(BF)
        act[rows, :] = active
        mlp[rows, :] = mm(active, second()).astype(BF)
        grad = mm_last(g[rows, :], second()) * (cdf + upper * pdf)
        grad_b = grad.astype(BF)
        gu[rows, :] = grad_b
        gbias[0, 0, :] += jnp.sum(grad_b.astype(F32), axis=0)
        gn2[rows, :] = mm_last(grad_b, first()).astype(BF)
        return carry

    lax.fori_loop(0, n2.shape[0] // TR, tile, 0)

    def grads(t, carry):
        cols = pl.ds(t * TG, TG)
        put_rows(keep_a, send_a, tab, 64, mine, t, mm_first(n2[:, cols], gu[...]))
        put_rows(keep_b, send_b, tab, 80, mine, t, mm_first(act[:, cols], g[...]))
        return carry

    lax.fori_loop(0, D // TG, grads, 0)


def mlp_part(tab, n2, g, bias, pieces_a, pieces_b, place, first_out, out_blocks, earlier):
    rows = n2.shape[0]
    vec = pl.BlockSpec((1, 1, D), lambda i: (i, 0, 0))
    half = pl.BlockSpec(HALF, lambda i: (0, first_out, 0, 0))
    part = jax.ShapeDtypeStruct((rows, D), BF)
    return pl.pallas_call(
        mlp_kernel,
        grid=(1,),
        in_specs=[smem(), const2((rows, D)), const2((rows, D)), vec]
        + pieces_at(lambda i: place) * 2
        + [pl.BlockSpec(memory_space=pl.ANY)] * len(earlier),
        out_specs=[half] * 4 + [const2((rows, D))] * 2 + [vec],
        out_shape=halves(out_blocks) + [part, part, jax.ShapeDtypeStruct((1, 1, D), F32)],
        scratch_shapes=[pltpu.VMEM((32, 32, D), BF)] * 2 + [pltpu.VMEM((rows, D), BF)] * 2,
        input_output_aliases={12 + p: p for p in range(len(earlier))},
        compiler_params=params(),
        cost_estimate=cost(12 * rows * D * D, 12 * D * D * 2, 2 * rows * D),
        name="mlp",
    )(tab, n2, g, bias, *pieces_a, *pieces_b, *earlier)


def locate(lengths, device_of, offsets, rows, which):
    row_ids = jnp.arange(rows, dtype=jnp.int32)
    inside = (
        (device_of[None, :] == which)
        & (row_ids[:, None] >= offsets[None, :])
        & (row_ids[:, None] < offsets[None, :] + lengths[None, :])
    ).astype(jnp.int32)
    found_any = jnp.sum(inside, axis=1)
    numbers = jnp.arange(lengths.shape[0], dtype=jnp.int32)
    segment = jnp.where(
        found_any > 0, jnp.sum(inside * numbers[None, :], axis=1), lengths.shape[0] + row_ids
    )
    position = jnp.where(found_any > 0, row_ids - jnp.sum(inside * offsets[None, :], axis=1), 0)
    return (segment, position)


def rotary_tables(position):
    lane = jnp.arange(128, dtype=jnp.int32)[None, :] % HD
    half_rot = ROT // 2
    exponent = (lane % half_rot).astype(F32) * (2.0 / ROT)
    angles = position.astype(F32)[:, None] * jnp.exp(-math.log(10000.0) * exponent)
    cosine, sine = jnp.cos(angles), jnp.sin(angles)
    return (
        jnp.where(lane < ROT, cosine, 1.0),
        jnp.where(lane < half_rot, sine, 0.0),
        jnp.where((lane >= half_rot) & (lane < ROT), sine, 0.0),
    )


def after(value, *others):
    return lax.optimization_barrier((value, others))[0]


class Chips:
    size = 32
    core = [(i, i ^ 1) for i in range(32)]
    x_way = [(i, i ^ 2) for i in range(32)]
    y_way = [(i, i ^ 4) for i in range(32)]
    z_ways = [[(i, (i + 8 * s) % 32) for i in range(32)] for s in range(4)]

    @staticmethod
    def table(me):
        z, y, x, c = me // 8, (me // 4) % 2, (me // 2) % 2, me % 2
        k = jnp.arange(32, dtype=jnp.int32)
        piece_c, piece_hi, mid, zr = k // 16, (k // 8) % 2, (k // 4) % 2, k % 4
        zz, cc = (z - zr) % 4, c ^ piece_c
        from_a = ((zz * 2 + (y ^ mid)) * 2 + (x ^ piece_hi)) * 2 + cc
        from_b = ((zz * 2 + (y ^ piece_hi)) * 2 + (x ^ mid)) * 2 + cc
        j = jnp.arange(16, dtype=jnp.int32)
        jz, jy, jx = (j // 4 - z) % 4, ((j // 2) % 2) ^ y, (j % 2) ^ x
        to_a = jx * 8 + jy * 4 + jz
        to_b = jy * 8 + jx * 4 + jz
        return jnp.concatenate([from_a, from_b, to_a, to_b, c[None]]).astype(jnp.int32)


def send(value, way):
    return lax.ppermute(value, "fsdp", way)


def beside(value, way, kernel):
    return after(send(value, way), kernel[-1])


def gather_z(shards):
    return [shards] + [send(shards, Chips.z_ways[s]) for s in (1, 2, 3)]


def stack_z(by_z, lo, hi):
    return jnp.stack([v[lo:hi] for v in by_z], axis=0)


def scatter_one(keep, got):
    total = lambda lo, hi: keep[lo:hi].astype(F32) + got[lo:hi].astype(F32)
    away = total(8, 16).astype(BF)
    return away, total


def scatter_two(total, got):
    more = lambda lo, hi: total(lo, hi) + got[lo:hi].astype(F32)
    return more(4, 8).astype(BF), more


def scatter_z(more_a, got_a, more_b, got_b):
    def at(s):
        a = more_a(s, s + 1)[0] + got_a[s].astype(F32)
        b = more_b(s, s + 1)[0] + got_b[s].astype(F32)
        return jnp.concatenate([a, b], axis=0)

    return at


def keep_whole(keep_a, send_a, keep_b, send_b):
    def one(keep, other):
        pairs = jnp.stack([keep, other], axis=1).transpose(2, 0, 1, 3, 4)
        return pairs.reshape(keep.shape[1], D, D).astype(F32)

    return one(keep_a, send_a), one(keep_b, send_b)


def gather_any(blocks):
    whole = lax.all_gather(blocks, "fsdp", axis=1, tiled=True)
    return in_pieces(whole.reshape(blocks.shape[0], 32, 32, D))


def in_pieces(whole):
    whole = whole.transpose(1, 0, 2, 3)
    return tuple(whole[8 * p : 8 * p + 8] for p in range(4))


def on_device(
    devices,
    tokens,
    out_cotangent,
    seq_lengths,
    seq_device,
    seq_offset,
    ln1_gain,
    ln1_bias,
    qkv_weight,
    qkv_bias,
    dense_weight,
    dense_bias,
    ln2_gain,
    ln2_bias,
    fc1_weight,
    fc1_bias,
    fc2_weight,
    fc2_bias,
):
    rows = tokens.shape[0]
    which = lax.axis_index("fsdp")
    chips = devices == Chips.size
    own_d = D // devices
    core, x_way, y_way, z_ways = Chips.core, Chips.x_way, Chips.y_way, Chips.z_ways

    vectors = (ln1_gain, ln1_bias, dense_bias, ln2_gain, ln2_bias, fc2_bias, qkv_bias, fc1_bias)
    packed = jnp.concatenate(vectors)
    packed = jnp.pad(packed, (0, -packed.shape[0] % 1024)).reshape(-1, 128)
    q_w, k_w, v_w = [qkv_weight[:, p * D : p * D + D] for p in range(3)]
    if chips:
        tab = Chips.table(which)
        fc1_shard = (
            fc1_weight.reshape(32, 32, 4, 32).transpose(2, 0, 1, 3).reshape(4, 32, D)
        )
        fc2_shard = fc2_weight.reshape(4, 32, D)
        z0 = gather_z(jnp.concatenate([fc1_shard[:1], fc2_shard[:1]], axis=0))
        z1 = gather_z(after(jnp.concatenate([fc1_shard[1:], fc2_shard[1:]], axis=0), *z0))
        vec4 = jnp.concatenate([v[None] for v in gather_z(after(packed, *z0))], axis=0)
        za, zb = stack_z(z0, 0, 1), stack_z(z0, 1, 2)
        near_a = jnp.concatenate([za, send(za, y_way)], axis=0)
        near_b = jnp.concatenate([zb, send(zb, x_way)], axis=0)
        vec8 = jnp.concatenate([vec4, send(vec4, y_way)], axis=0)
        far_a, far_b = send(near_a, x_way), send(near_b, y_way)
        vec16 = jnp.concatenate([vec8, send(vec8, x_way)], axis=0)
        m0_a = (near_a, far_a, send(near_a, core), send(far_a, core))
        m0_b = (near_b, far_b, send(near_b, core), send(far_b, core))
        vec32 = jnp.concatenate([vec16, send(vec16, core)], axis=0)
        places = jnp.arange(32, dtype=jnp.int32)
        pick = (tab[None, :32] == places[:, None]).astype(BF)
        packed = mm(pick, vec32.reshape(32, -1))
    else:
        ident = jnp.arange(32, dtype=jnp.int32)
        tab = jnp.concatenate([ident, ident, ident[:16], ident[:16], ident[:1]])
        packed = lax.all_gather(packed, "fsdp", axis=0, tiled=True).reshape(devices, -1)
        packed = packed.astype(F32)
        fc1 = gather_any(fc1_weight.reshape(own_d, 4, D).transpose(1, 0, 2))
        fc2 = lax.all_gather(fc2_weight, "fsdp", axis=0, tiled=True)
        fc2 = in_pieces(fc2.reshape(4, 32, 32, D))
        m0_a, m1_a = tuple(w[:, :1] for w in fc1), tuple(w[:, 1:] for w in fc1)
        m0_b, m1_b = tuple(w[:, :1] for w in fc2), tuple(w[:, 1:] for w in fc2)
        t_a = gather_any(jnp.stack([q_w, dense_weight]))
        t_b = gather_any(jnp.stack([k_w, v_w]))

    full, at = [], 0
    for v in vectors:
        full.append(packed[:, at : at + v.shape[0]])
        at += v.shape[0]
    gain1, bias1, dense_b, gain2, bias2, fc2_b, qkv_b = [v.reshape(-1) for v in full[:7]]
    qkv_b = qkv_b.reshape(3, 1, D)
    if chips:
        fc1_b = full[7].reshape(32, 4, 32).transpose(1, 0, 2).reshape(4, 1, D)
    else:
        fc1_b = full[7].reshape(4, 1, D)

    if chips:
        tokens, out_cotangent, seq_lengths, seq_device, seq_offset = after(
            (tokens, out_cotangent, seq_lengths, seq_device, seq_offset), near_a, near_b
        )
    segment, position = locate(seq_lengths, seq_device, seq_offset, rows, which)
    tables = rotary_tables(position)
    rows_in = tokens.astype(F32)
    row_mean = jnp.mean(rows_in, axis=-1, keepdims=True)
    centred = rows_in - row_mean
    row_var = jnp.mean(centred * centred, axis=-1, keepdims=True)
    scale = lax.rsqrt(row_var + EPSILON)
    normal = centred * scale
    n1 = (normal * gain1 + bias1).astype(BF)
    n2 = (normal * gain2 + bias2).astype(BF)
    grad_out = out_cotangent.astype(F32)
    cotangent_sum = jnp.sum(grad_out, axis=0)
    g = out_cotangent
    seg_col, seg_row = segment[:, None], segment[None, :]

    def mlp(data, block, pieces, place, earlier):
        return mlp_part(
            tab, data, g, fc1_b[block : block + 1], *pieces, place, block % 2, 2, earlier
        )

    if chips:
        za, zb = after((stack_z(z1, 0, 3), stack_z(z1, 3, 6)), near_a, near_b)
        near_a = jnp.concatenate([za, send(za, y_way)], axis=0)
        near_b = jnp.concatenate([zb, send(zb, x_way)], axis=0)
        t_shards = after(jnp.stack([q_w, dense_weight, k_w, v_w]), near_a, near_b)
        start = after(n2, near_a, near_b, t_shards, n1, tables, seg_col, seg_row, qkv_b)
        r0 = mlp(start, 0, (m0_a, m0_b), 0, ())
        far_a, far_b = beside(near_a, x_way, r0), beside(near_b, y_way, r0)
        zt = gather_z(after(t_shards, far_a, far_b))
        m1_a = (near_a, far_a, send(near_a, core), send(far_a, core))
        m1_b = (near_b, far_b, send(near_b, core), send(far_b, core))
        r1 = mlp(after(n2, r0[4]), 1, (m1_a, m1_b), 0, r0[:4])
        zt = [zt[0], *after(zt[1:], r1[4])]
        za, zb = stack_z(zt, 0, 2), stack_z(zt, 2, 4)
        r2 = mlp(after(n2, za, zb, r1[4]), 2, (m1_a, m1_b), 1, ())
        near_a = jnp.concatenate([za, beside(za, y_way, r2)], axis=0)
        near_b = jnp.concatenate([zb, beside(zb, x_way, r2)], axis=0)
        got_a, got_b = beside(r1[1], core, r2), beside(r1[3], core, r2)
        r3 = mlp(after(n2, near_a, near_b, got_a, got_b, r2[4]), 3, (m1_a, m1_b), 2, r2[:4])
        far_a, far_b = beside(near_a, x_way, r3), beside(near_b, y_way, r3)
        t_a = (near_a, far_a, send(near_a, core), send(far_a, core))
        t_b = (near_b, far_b, send(near_b, core), send(far_b, core))
        keep = after((r1[0], r1[2]), r3[4])
        away_a, sum_a = scatter_one(keep[0], got_a)
        away_b, sum_b = scatter_one(keep[1], got_b)
        qkvd = project(tab, after(n1, away_a, away_b, r3[4]), g, qkv_b, tables, t_a, t_b)
        got_a, got_b = beside(away_a, x_way, [qkvd]), beside(away_b, y_way, [qkvd])
        far2_a, far2_b = beside(r3[1], core, [qkvd]), beside(r3[3], core, [qkvd])
        away_a, more_a = scatter_two(sum_a, got_a)
        away_b, more_b = scatter_two(sum_b, got_b)
        away2_a, sum2_a = scatter_one(r3[0], far2_a)
        away2_b, sum2_b = scatter_one(r3[2], far2_b)
        first = attention(
            seg_col, seg_row, tables, after(qkvd, away_a, away_b, away2_a, away2_b), 0, 4, ()
        )
        got_a, got_b = beside(away_a, y_way, first), beside(away_b, x_way, first)
        got2_a, got2_b = beside(away2_a, x_way, first), beside(away2_b, y_way, first)
        z_part = scatter_z(more_a, got_a, more_b, got_b)
        z_away = [z_part(s).astype(BF) for s in (1, 2, 3)]
        away2_a, more2_a = scatter_two(sum2_a, got2_a)
        away2_b, more2_b = scatter_two(sum2_b, got2_b)
        second = attention(
            seg_col, seg_row, tables, after(qkvd, z_away, away2_a, away2_b), 4, 4, first
        )
        mixed, dq, dk, dv = second
        z_got = [beside(v, z_ways[s + 1], second) for s, v in enumerate(z_away)]
        got2_a, got2_b = beside(away2_a, y_way, second), beside(away2_b, x_way, second)
        z_part2 = scatter_z(more2_a, got2_a, more2_b, got2_b)
        z_away2 = [z_part2(s).astype(BF) for s in (1, 2, 3)]
        b1 = dense_value(tab, after(n1, z_away2, z_got), g, mixed, dv, t_a, t_b)
        z_got2 = [beside(v, z_ways[s + 1], b1) for s, v in enumerate(z_away2)]
        got_a, got_b = send(b1[1], core), send(b1[3], core)
        away_a, sum_a = scatter_one(b1[0], got_a)
        away_b, sum_b = scatter_one(b1[2], got_b)
        b2 = query_key(tab, after(n1, away_a, away_b), dq, dk, t_a, t_b)
        got_a, got_b = beside(away_a, x_way, b2), beside(away_b, y_way, b2)
        got2_a, got2_b = send(b2[1], core), send(b2[3], core)
        away2_a, sum2_a = scatter_one(b2[0], got2_a)
        away2_b, sum2_b = scatter_one(b2[2], got2_b)
        away_a, more_a = scatter_two(sum_a, got_a)
        away_b, more_b = scatter_two(sum_b, got_b)
        gn_parts = after(
            [b1[5], b2[4]] + [r[5] for r in (r0, r1, r2, r3)], away2_a, away2_b, away_a, away_b
        )
    else:
        r0 = mlp(n2, 0, (m0_a, m0_b), 0, ())
        r1 = mlp(n2, 1, (m1_a, m1_b), 0, r0[:4])
        r2 = mlp(n2, 2, (m1_a, m1_b), 1, ())
        r3 = mlp(n2, 3, (m1_a, m1_b), 2, r2[:4])
        qkvd = project(tab, n1, g, qkv_b, tables, t_a, t_b)
        first = attention(seg_col, seg_row, tables, qkvd, 0, 4, ())
        mixed, dq, dk, dv = attention(seg_col, seg_row, tables, qkvd, 4, 4, first)
        b1 = dense_value(tab, n1, g, mixed, dv, t_a, t_b)
        b2 = query_key(tab, n1, dq, dk, t_a, t_b)
        gn_parts = [b1[5], b2[4]] + [r[5] for r in (r0, r1, r2, r3)]

    gn_parts = [v.astype(F32) for v in gn_parts]
    gn1, gn2 = gn_parts[0] + gn_parts[1], sum(gn_parts[2:])
    out_parts = [b1[4], r0[4], r1[4], r2[4], r3[4]]
    grad_ln1_g = jnp.sum(gn1 * normal, axis=0)
    grad_ln1_b = jnp.sum(gn1, axis=0)
    grad_ln2_g = jnp.sum(gn2 * normal, axis=0)
    grad_ln2_b = jnp.sum(gn2, axis=0)
    gqkv_b = jnp.concatenate([b2[5], b1[6]], axis=0)
    gfc1_b = jnp.concatenate([r0[6], r1[6], r2[6], r3[6]], axis=0)[:, 0]
    if chips:
        gfc1_b = gfc1_b.reshape(4, 32, 32).transpose(1, 0, 2)
    small = [
        v.reshape(devices, -1)
        for v in (grad_ln1_g, grad_ln1_b, cotangent_sum, grad_ln2_g, grad_ln2_b, gqkv_b, gfc1_b)
    ]
    joint = jnp.concatenate(small, axis=1)
    if chips:
        j = places // 2
        slot = ((places % 2) ^ (which % 2)) * 16 + jnp.take(tab[64:80], j)
        to_slot = (slot[None, :] == places[:, None]).astype(F32)
        vec = jnp.dot(to_slot, joint, precision=lax.Precision.HIGHEST)
    if chips:
        got2_a, got2_b = send(away2_a, x_way), send(away2_b, y_way)
        away2_a, more2_a = scatter_two(sum2_a, got2_a)
        away2_b, more2_b = scatter_two(sum2_b, got2_b)
        got_a, got_b = send(away_a, y_way), send(away_b, x_way)
        z_b1 = scatter_z(more_a, got_a, more_b, got_b)
        z_away = [z_b1(s).astype(BF) for s in (1, 2, 3)]
        away2_a, away2_b = after((away2_a, away2_b), z_away)
        got2_a, got2_b = send(away2_a, y_way), send(away2_b, x_way)
        z_got_b1 = [send(v, z_ways[s + 1]) for s, v in enumerate(z_away)]
        z_b2 = scatter_z(more2_a, got2_a, more2_b, got2_b)
        z_away2 = [z_b2(s).astype(BF) for s in (1, 2, 3)]
        out_parts = after(out_parts, z_away2)
        joint = after(vec, z_away2)
        joint = joint[:16] + send(joint[16:], core)
        joint = joint[:8] + send(joint[8:], x_way)
        joint = joint[:4] + send(joint[4:], y_way)
        owned = joint[0] + sum(send(joint[s], z_ways[s]) for s in (1, 2, 3))
    else:
        joint = jnp.pad(joint, ((0, 0), (0, -joint.shape[1] % 1024))).reshape(-1, 128)
        owned = lax.psum_scatter(joint, "fsdp", scatter_dimension=0, tiled=True).reshape(-1)
    out, at = [], 0
    for v in small:
        out.append(owned[at : at + v.shape[1]])
        at += v.shape[1]
    o_ln1_g, o_ln1_b, o_cot, o_ln2_g, o_ln2_b, o_qkv_b, o_fc1_b = out

    result = (rows_in + sum(v.astype(F32) for v in out_parts) + dense_b + fc2_b).astype(BF)
    into = gn1 * gain1 + gn2 * gain2
    if chips:
        into, part0, part1 = after((into, z_part(0), z_part2(0)), z_away2)
        own0 = part0 + sum(v.astype(F32) for v in z_got)
        own1 = part1 + sum(v.astype(F32) for v in z_got2)
        own_b1 = z_b1(0) + sum(v.astype(F32) for v in z_got_b1)
        g_fc1 = jnp.concatenate([own0[:2], own1[:2]], axis=0)
        g_fc2 = jnp.concatenate([own0[2:], own1[2:]], axis=0)
        g_fc1 = g_fc1.reshape(4, 32, 32, 32).transpose(1, 2, 0, 3).reshape(32, FF)
        g_fc2 = g_fc2.reshape(128, D)
        own_b2 = z_b2(0) + sum(
            send(v, z_ways[s + 1]).astype(F32) for s, v in enumerate(z_away2)
        )
        g_t = (own_b2[0], own_b2[1], own_b1[1], own_b1[0])
    else:
        first, second = keep_whole(*r1[:4]), keep_whole(*r3[:4])
        g_fc1 = jnp.concatenate([first[0], second[0]], axis=0)
        g_fc2 = jnp.concatenate([first[1], second[1]], axis=0)
        g_fc1 = lax.psum_scatter(g_fc1, "fsdp", scatter_dimension=1, tiled=True)
        g_fc1 = g_fc1.transpose(1, 0, 2).reshape(own_d, FF)
        g_fc2 = lax.psum_scatter(
            g_fc2.reshape(FF, D), "fsdp", scatter_dimension=0, tiled=True
        )
        dense_part, value_part = keep_whole(*b1[:4])
        g_t = lax.psum_scatter(
            jnp.concatenate([*keep_whole(*b2[:4]), value_part, dense_part], axis=0),
            "fsdp", scatter_dimension=1, tiled=True,
        )
    g_qkv = jnp.concatenate(g_t[:3], axis=1)
    g_dense = g_t[3]

    back = scale * (
        into
        - jnp.mean(into, axis=-1, keepdims=True)
        - normal * jnp.mean(into * normal, axis=-1, keepdims=True)
    )
    grad_tokens = (grad_out + back).astype(BF)
    return (
        result, grad_tokens, o_ln1_g, o_ln1_b, g_qkv, o_qkv_b, g_dense, o_cot,
        o_ln2_g, o_ln2_b, g_fc1, o_fc1_b, g_fc2, o_cot,
    )


def solution(mesh):
    rows, vec, whole = P("fsdp", None), P("fsdp"), P()
    return jax.shard_map(
        partial(on_device, mesh.shape["fsdp"]),
        mesh=mesh,
        in_specs=(
            rows, rows, whole, whole, whole, vec, vec, rows, vec, rows, vec, vec, vec,
            rows, vec, rows, vec,
        ),
        out_specs=(
            rows, rows, vec, vec, rows, vec, rows, vec, vec, vec, rows, vec, rows, vec,
        ),
        check_vma=False,
    )
```

```python
from functools import partial
import math

import jax
import jax.numpy as jnp
from jax import lax
from jax.experimental import pallas as pl
from jax.experimental.pallas import tpu as pltpu
from jax.sharding import PartitionSpec as P

D = 1024
H = 16
HD = 64
ROT = 16
FF = 4096

EPSILON = 1e-05
MASKED = -1e30
BF = jnp.bfloat16
F32 = jnp.float32
LAST = (((1,), (1,)), ((), ()))
FIRST = (((0,), (0,)), ((), ()))
VMEM_LIMIT = 60 * 1024 * 1024


def mm(a, b):
    return jnp.dot(a, b, preferred_element_type=F32)


def mm_last(a, b):
    return lax.dot_general(a, b, LAST, preferred_element_type=F32)


def mm_first(a, b):
    return lax.dot_general(a, b, FIRST, preferred_element_type=F32)


def assemble(w_scr, pieces, tab, base):
    for p, piece in enumerate(pieces):
        for j in range(8):
            w_scr[tab[base + p * 8 + j]] = piece[j, 0]


def put_rows(keep_ref, send_ref, tab, base, mine, tile, values):
    pairs = values.shape[0] // 64
    blocks = values.astype(BF).reshape(pairs, 2, 32, values.shape[1])
    even, odd = blocks[:, 0], blocks[:, 1]
    keep = jnp.where(mine == 0, even, odd)
    send = jnp.where(mine == 0, odd, even)
    for j in range(pairs):
        slot = tab[base + tile * pairs + j]
        keep_ref[slot, 0] = keep[j]
        send_ref[slot, 0] = send[j]


def turn(x, cosine, sine_a, sine_b, sign):
    left = pltpu.roll(x, x.shape[1] - ROT // 2, 1)
    right = pltpu.roll(x, ROT // 2, 1)
    return x * cosine - sign * (left * sine_a - right * sine_b)


TR = 1024
TG = 1024


def project_kernel(tab, n1, g, bias, cos, sa, sb, *refs):
    pa, pb, out, w_scr = refs[:4], refs[4:8], refs[8], refs[9]
    i = pl.program_id(0)
    from_b = (i == 1) | (i == 2)

    @pl.when(jnp.logical_not(from_b))
    def _():
        assemble(w_scr, pa, tab, 0)

    @pl.when(from_b)
    def _():
        assemble(w_scr, pb, tab, 32)

    def weight():
        return w_scr[...].reshape(D, D)

    @pl.when(i < 2)
    def _():
        def tile(t, carry):
            rows = pl.ds(t * TR, TR)
            val = mm(n1[rows, :], weight()) + bias[0].astype(F32)
            c, a, b = cos[rows, :], sa[rows, :], sb[rows, :]
            for j in range(D // 128):
                cols = slice(j * 128, j * 128 + 128)
                out[0, rows, cols] = turn(val[:, cols], c, a, b, 1.0).astype(BF)
            return carry

        lax.fori_loop(0, D // TR, tile, 0)

    @pl.when(i == 2)
    def _():
        def tile(t, carry):
            rows = pl.ds(t * TR, TR)
            out[0, rows, :] = (mm(n1[rows, :], weight()) + bias[0].astype(F32)).astype(BF)
            return carry

        lax.fori_loop(0, D // TR, tile, 0)

    @pl.when(i == 3)
    def _():
        def tile(t, carry):
            rows = pl.ds(t * TR, TR)
            out[0, rows, :] = mm_last(g[rows, :], weight()).astype(BF)
            return carry

        lax.fori_loop(0, D // TR, tile, 0)


def const2(shape):
    return pl.BlockSpec(shape, lambda i: (0,) * len(shape))


def smem():
    return pl.BlockSpec(memory_space=pltpu.SMEM)


def params():
    return pltpu.CompilerParams(
        dimension_semantics=("arbitrary",), vmem_limit_bytes=VMEM_LIMIT
    )


def cost(flops, bytes_accessed, transcendentals=0):
    return pl.CostEstimate(
        flops=flops, bytes_accessed=bytes_accessed, transcendentals=transcendentals
    )


PIECE = (8, 1, 32, D)
HALF = (16, 1, 32, D)


def pieces_at(place):
    return [pl.BlockSpec(PIECE, lambda i: (0, place(i), 0, 0))] * 4


def project(tab, n1, g, bias, tables, pieces_a, pieces_b):
    rows = n1.shape[0]
    return pl.pallas_call(
        project_kernel,
        grid=(4,),
        in_specs=[smem(), const2((rows, D)), const2((rows, D)),
                  pl.BlockSpec((1, 1, D), lambda i: (jnp.minimum(i, 2), 0, 0))]
        + [const2((rows, 128))] * 3 + pieces_at(lambda i: i // 3)
        + pieces_at(lambda i: i // 2),
        out_specs=pl.BlockSpec((1, rows, D), lambda i: (i, 0, 0)),
        out_shape=jax.ShapeDtypeStruct((4, rows, D), BF),
        scratch_shapes=[pltpu.VMEM((32, 32, D), BF)],
        compiler_params=params(),
        cost_estimate=cost(8 * rows * D * D, 20 * D * D),
        name="project",
    )(tab, n1, g, bias, *tables, *pieces_a, *pieces_b)


AQ = 256


def attention_kernel(segc, segr, cos, sa, sb, q, k, v, dm, *refs):
    mixed, dq, dk, dv, mask, dk_acc, dv_acc = refs[-7:]
    rows = q.shape[1]
    step = pl.program_id(0)

    @pl.when(step == 0)
    def _():
        for r in range(0, rows, AQ):
            n = r + AQ
            row_ids = r + lax.broadcasted_iota(jnp.int32, (AQ, n), 0)
            col_ids = lax.broadcasted_iota(jnp.int32, (AQ, n), 1)
            ok = (segc[r:r + AQ, :] == segr[:, :n]) & (col_ids <= row_ids)
            mask[r:r + AQ, :n] = jnp.where(ok, 0.0, MASKED)

    lane = lax.broadcasted_iota(jnp.int32, (1, 128), 1)
    dk_acc[...] = jnp.zeros_like(dk_acc)
    dv_acc[...] = jnp.zeros_like(dv_acc)
    zero = jnp.zeros((), BF)
    for r in range(0, rows, AQ):
        n = r + AQ
        blk = slice(r, r + AQ)
        mixed_sum = jnp.zeros((AQ, 128), F32)
        dq_sum = jnp.zeros((AQ, 128), F32)
        for h in range(2):
            own = (lane < 64) if h == 0 else (lane >= 64)
            kk, vv = k[0, :n, :], v[0, :n, :]
            qh = jnp.where(own, q[0, blk, :] * jnp.asarray(HD ** -0.5, BF), zero)
            dmh = jnp.where(own, dm[0, blk, :], zero)
            s = mm_last(qh, kk) + mask[blk, :n]
            top = jnp.max(s, axis=1, keepdims=True)
            e = jnp.exp(s - top)
            p = e * (1.0 / jnp.sum(e, axis=1, keepdims=True))
            pb = p.astype(BF)
            dp = mm_last(dmh, vv)
            delta = jnp.sum(p * dp, axis=1, keepdims=True)
            ds = (p * (dp - delta)).astype(BF)
            mixed_sum += mm(pb, jnp.where(own, vv, zero))
            dq_sum += mm(ds, jnp.where(own, kk, zero))
            dk_acc[:n, :] += mm_first(ds, qh)
            dv_acc[:n, :] += mm_first(pb, dmh)
        mixed[blk, :] = mixed_sum.astype(BF)
        dq[0, blk, :] = turn(
            dq_sum * HD ** -0.5, cos[blk, :], sa[blk, :], sb[blk, :], -1.0
        ).astype(BF)
    dk[0, :, :] = turn(dk_acc[...], cos[...], sa[...], sb[...], -1.0).astype(BF)
    dv[0, :, :] = dv_acc[...].astype(BF)


def attention(seg_col, seg_row, tables, qkvd, first, steps, earlier):
    rows = qkvd.shape[1]

    def part(p):
        return pl.BlockSpec((1, rows, 128), lambda i: (p, 0, i + first))

    def out3():
        return pl.BlockSpec((1, rows, 128), lambda i: (0, 0, i + first))

    return pl.pallas_call(
        attention_kernel,
        grid=(steps,),
        in_specs=[const2((rows, 1)), const2((1, rows))] + [const2((rows, 128))] * 3
        + [part(p) for p in range(4)] + [pl.BlockSpec(memory_space=pl.ANY)] * len(earlier),
        out_specs=[pl.BlockSpec((rows, 128), lambda i: (0, i + first))] + [out3()] * 3,
        out_shape=[jax.ShapeDtypeStruct((rows, D), BF)]
        + [jax.ShapeDtypeStruct((1, rows, D), BF)] * 3,
        scratch_shapes=[pltpu.VMEM((rows, rows), F32), pltpu.VMEM((rows, 128), F32),
                        pltpu.VMEM((rows, 128), F32)],
        input_output_aliases={9 + p: p for p in range(len(earlier))},
        compiler_params=params(),
        cost_estimate=cost(3 * steps * rows * rows * D, 2 * steps * rows * D,
                           2 * steps * rows * rows),
        name="attention",
    )(seg_col, seg_row, *tables, qkvd, qkvd, qkvd, qkvd, *earlier)


def weight_grad(left, right, keep, send, tab, base):
    def tile(t, carry):
        val = mm_first(left[:, pl.ds(t * TG, TG)], right)
        put_rows(keep, send, tab, base, tab[96], t, val)
        return carry

    lax.fori_loop(0, D // TG, tile, 0)


def input_grad(gj, weight, out, add=None):
    def tile(t, carry):
        rows = pl.ds(t * TR, TR)
        val = mm_last(gj[rows, :], weight())
        val = val if add is None else add[rows, :] + val
        out[rows, :] = val.astype(out.dtype)
        return carry

    lax.fori_loop(0, gj.shape[0] // TR, tile, 0)


def dense_value_kernel(tab, n1, g, mixed, dv, *refs):
    pa, pb = refs[:4], refs[4:8]
    keep_a, send_a, keep_b, send_b, attn, gn1, bias, w_scr = refs[8:]

    def weight():
        return w_scr[...].reshape(D, D)

    @pl.when(pl.program_id(0) == 0)
    def _():
        assemble(w_scr, pa, tab, 0)

        def tile(t, carry):
            rows = pl.ds(t * TR, TR)
            attn[rows, :] = mm(mixed[rows, :], weight()).astype(BF)
            return carry

        lax.fori_loop(0, mixed.shape[0] // TR, tile, 0)
        weight_grad(mixed, g[...], keep_a, send_a, tab, 64)

    @pl.when(pl.program_id(0) == 1)
    def _():
        assemble(w_scr, pb, tab, 32)
        bias[0, 0, :] = jnp.sum(dv[0].astype(F32), axis=0)
        input_grad(dv.at[0], weight, gn1)
        weight_grad(n1, dv[0], keep_b, send_b, tab, 80)


def query_key_kernel(tab, n1, dq, dk, *refs):
    pa, pb = refs[:4], refs[4:8]
    keep_a, send_a, keep_b, send_b, gn1, bias, w_scr, gn1_scr = refs[8:]

    def weight():
        return w_scr[...].reshape(D, D)

    @pl.when(pl.program_id(0) == 0)
    def _():
        assemble(w_scr, pa, tab, 0)
        bias[0, 0, :] = jnp.sum(dq[0].astype(F32), axis=0)
        input_grad(dq.at[0], weight, gn1_scr)
        weight_grad(n1, dq[0], keep_a, send_a, tab, 64)

    @pl.when(pl.program_id(0) == 1)
    def _():
        assemble(w_scr, pb, tab, 32)
        bias[1, 0, :] = jnp.sum(dk[0].astype(F32), axis=0)
        input_grad(dk.at[0], weight, gn1, gn1_scr)
        weight_grad(n1, dk[0], keep_b, send_b, tab, 80)


def halves(blocks):
    return [jax.ShapeDtypeStruct((16, blocks, 32, D), BF)] * 4


def dense_value(tab, n1, g, mixed, dv, pieces_a, pieces_b):
    rows = n1.shape[0]
    full = jax.ShapeDtypeStruct((rows, D), BF)
    return pl.pallas_call(
        dense_value_kernel,
        grid=(2,),
        in_specs=[smem()] + [const2((rows, D))] * 3 + [const2((1, rows, D))]
        + pieces_at(lambda i: 1) + pieces_at(lambda i: 1),
        out_specs=[const2(HALF)] * 4 + [const2((rows, D))] * 2 + [const2((1, 1, D))],
        out_shape=halves(1) + [full, full, jax.ShapeDtypeStruct((1, 1, D), F32)],
        scratch_shapes=[pltpu.VMEM((32, 32, D), BF)],
        compiler_params=params(),
        cost_estimate=cost(8 * rows * D * D, 20 * D * D),
        name="dense_value",
    )(tab, n1, g, mixed, dv, *pieces_a, *pieces_b)


def query_key(tab, n1, dq, dk, pieces_a, pieces_b):
    rows = n1.shape[0]
    full = jax.ShapeDtypeStruct((rows, D), BF)
    return pl.pallas_call(
        query_key_kernel,
        grid=(2,),
        in_specs=[smem(), const2((rows, D))] + [const2((1, rows, D))] * 2
        + pieces_at(lambda i: 0) + pieces_at(lambda i: 0),
        out_specs=[const2(HALF)] * 4 + [const2((rows, D)), const2((2, 1, D))],
        out_shape=halves(1) + [full, jax.ShapeDtypeStruct((2, 1, D), F32)],
        scratch_shapes=[pltpu.VMEM((32, 32, D), BF), pltpu.VMEM((rows, D), F32)],
        compiler_params=params(),
        cost_estimate=cost(8 * rows * D * D, 20 * D * D),
        name="query_key",
    )(tab, n1, dq, dk, *pieces_a, *pieces_b)


def mlp_kernel(tab, n2, g, bias, *refs):
    pa, pb = refs[:4], refs[4:8]
    keep_a, send_a, keep_b, send_b, mlp, gn2, gbias = refs[-11:-4]
    w1_scr, w2_scr, act, gu = refs[-4:]
    mine = tab[96]
    assemble(w1_scr, pa, tab, 0)
    assemble(w2_scr, pb, tab, 32)

    def first():
        return w1_scr[...].reshape(D, D)

    def second():
        return w2_scr[...].reshape(D, D)

    gbias[...] = jnp.zeros_like(gbias)

    def tile(t, carry):
        rows = pl.ds(t * TR, TR)
        upper = mm(n2[rows, :], first()) + bias[0].astype(F32)
        cdf = 0.5 * (1.0 + lax.erf(upper * 2.0 ** -0.5))
        pdf = jnp.exp(-0.5 * upper * upper) * (2.0 * math.pi) ** -0.5
        active = (upper * cdf).astype(BF)
        act[rows, :] = active
        mlp[rows, :] = mm(active, second()).astype(BF)
        grad = mm_last(g[rows, :], second()) * (cdf + upper * pdf)
        grad_b = grad.astype(BF)
        gu[rows, :] = grad_b
        gbias[0, 0, :] += jnp.sum(grad_b.astype(F32), axis=0)
        gn2[rows, :] = mm_last(grad_b, first()).astype(BF)
        return carry

    lax.fori_loop(0, n2.shape[0] // TR, tile, 0)

    def grads(t, carry):
        cols = pl.ds(t * TG, TG)
        put_rows(keep_a, send_a, tab, 64, mine, t, mm_first(n2[:, cols], gu[...]))
        put_rows(keep_b, send_b, tab, 80, mine, t, mm_first(act[:, cols], g[...]))
        return carry

    lax.fori_loop(0, D // TG, grads, 0)


def mlp_part(tab, n2, g, bias, pieces_a, pieces_b, place, first_out, out_blocks, earlier):
    rows = n2.shape[0]
    vec = pl.BlockSpec((1, 1, D), lambda i: (i, 0, 0))
    half = pl.BlockSpec(HALF, lambda i: (0, first_out, 0, 0))
    part = jax.ShapeDtypeStruct((rows, D), BF)
    return pl.pallas_call(
        mlp_kernel,
        grid=(1,),
        in_specs=[smem(), const2((rows, D)), const2((rows, D)), vec]
        + pieces_at(lambda i: place) * 2
        + [pl.BlockSpec(memory_space=pl.ANY)] * len(earlier),
        out_specs=[half] * 4 + [const2((rows, D))] * 2 + [vec],
        out_shape=halves(out_blocks) + [part, part, jax.ShapeDtypeStruct((1, 1, D), F32)],
        scratch_shapes=[pltpu.VMEM((32, 32, D), BF)] * 2 + [pltpu.VMEM((rows, D), BF)] * 2,
        input_output_aliases={12 + p: p for p in range(len(earlier))},
        compiler_params=params(),
        cost_estimate=cost(12 * rows * D * D, 12 * D * D * 2, 2 * rows * D),
        name="mlp",
    )(tab, n2, g, bias, *pieces_a, *pieces_b, *earlier)


def locate(lengths, device_of, offsets, rows, which):
    row_ids = jnp.arange(rows, dtype=jnp.int32)
    inside = (
        (device_of[None, :] == which)
        & (row_ids[:, None] >= offsets[None, :])
        & (row_ids[:, None] < offsets[None, :] + lengths[None, :])
    ).astype(jnp.int32)
    found_any = jnp.sum(inside, axis=1)
    numbers = jnp.arange(lengths.shape[0], dtype=jnp.int32)
    segment = jnp.where(
        found_any > 0, jnp.sum(inside * numbers[None, :], axis=1), lengths.shape[0] + row_ids
    )
    position = jnp.where(found_any > 0, row_ids - jnp.sum(inside * offsets[None, :], axis=1), 0)
    return (segment, position)


def rotary_tables(position):
    lane = jnp.arange(128, dtype=jnp.int32)[None, :] % HD
    half_rot = ROT // 2
    exponent = (lane % half_rot).astype(F32) * (2.0 / ROT)
    angles = position.astype(F32)[:, None] * jnp.exp(-math.log(10000.0) * exponent)
    cosine, sine = jnp.cos(angles), jnp.sin(angles)
    return (
        jnp.where(lane < ROT, cosine, 1.0),
        jnp.where(lane < half_rot, sine, 0.0),
        jnp.where((lane >= half_rot) & (lane < ROT), sine, 0.0),
    )


def after(value, *others):
    return lax.optimization_barrier((value, others))[0]


class Chips:
    size = 32
    core = [(i, i ^ 1) for i in range(32)]
    x_way = [(i, i ^ 2) for i in range(32)]
    y_way = [(i, i ^ 4) for i in range(32)]
    z_ways = [[(i, (i + 8 * s) % 32) for i in range(32)] for s in range(4)]

    @staticmethod
    def table(me):
        z, y, x, c = me // 8, (me // 4) % 2, (me // 2) % 2, me % 2
        k = jnp.arange(32, dtype=jnp.int32)
        piece_c, piece_hi, mid, zr = k // 16, (k // 8) % 2, (k // 4) % 2, k % 4
        zz, cc = (z - zr) % 4, c ^ piece_c
        from_a = ((zz * 2 + (y ^ mid)) * 2 + (x ^ piece_hi)) * 2 + cc
        from_b = ((zz * 2 + (y ^ piece_hi)) * 2 + (x ^ mid)) * 2 + cc
        j = jnp.arange(16, dtype=jnp.int32)
        jz, jy, jx = (j // 4 - z) % 4, ((j // 2) % 2) ^ y, (j % 2) ^ x
        to_a = jx * 8 + jy * 4 + jz
        to_b = jy * 8 + jx * 4 + jz
        return jnp.concatenate([from_a, from_b, to_a, to_b, c[None]]).astype(jnp.int32)


def send(value, way):
    return lax.ppermute(value, "fsdp", way)


def beside(value, way, kernel):
    return after(send(value, way), kernel[-1])


def gather_z(shards):
    return [shards] + [send(shards, Chips.z_ways[s]) for s in (1, 2, 3)]


def stack_z(by_z, lo, hi):
    return jnp.stack([v[lo:hi] for v in by_z], axis=0)


def scatter_one(keep, got):
    total = lambda lo, hi: keep[lo:hi].astype(F32) + got[lo:hi].astype(F32)
    away = total(8, 16).astype(BF)
    return away, total


def scatter_two(total, got):
    more = lambda lo, hi: total(lo, hi) + got[lo:hi].astype(F32)
    return more(4, 8).astype(BF), more


def scatter_z(more_a, got_a, more_b, got_b):
    def at(s):
        a = more_a(s, s + 1)[0] + got_a[s].astype(F32)
        b = more_b(s, s + 1)[0] + got_b[s].astype(F32)
        return jnp.concatenate([a, b], axis=0)

    return at


def keep_whole(keep_a, send_a, keep_b, send_b):
    def one(keep, other):
        pairs = jnp.stack([keep, other], axis=1).transpose(2, 0, 1, 3, 4)
        return pairs.reshape(keep.shape[1], D, D).astype(F32)

    return one(keep_a, send_a), one(keep_b, send_b)


def gather_any(blocks):
    whole = lax.all_gather(blocks, "fsdp", axis=1, tiled=True)
    return in_pieces(whole.reshape(blocks.shape[0], 32, 32, D))


def in_pieces(whole):
    whole = whole.transpose(1, 0, 2, 3)
    return tuple(whole[8 * p : 8 * p + 8] for p in range(4))


def on_device(
    devices,
    tokens,
    out_cotangent,
    seq_lengths,
    seq_device,
    seq_offset,
    ln1_gain,
    ln1_bias,
    qkv_weight,
    qkv_bias,
    dense_weight,
    dense_bias,
    ln2_gain,
    ln2_bias,
    fc1_weight,
    fc1_bias,
    fc2_weight,
    fc2_bias,
):
    rows = tokens.shape[0]
    which = lax.axis_index("fsdp")
    chips = devices == Chips.size
    own_d = D // devices
    core, x_way, y_way, z_ways = Chips.core, Chips.x_way, Chips.y_way, Chips.z_ways

    vectors = (ln1_gain, ln1_bias, dense_bias, ln2_gain, ln2_bias, fc2_bias, qkv_bias, fc1_bias)
    packed = jnp.concatenate(vectors)
    packed = jnp.pad(packed, (0, -packed.shape[0] % 1024)).reshape(-1, 128)
    q_w, k_w, v_w = [qkv_weight[:, p * D : p * D + D] for p in range(3)]
    if chips:
        tab = Chips.table(which)
        fc1_shard = (
            fc1_weight.reshape(32, 32, 4, 32).transpose(2, 0, 1, 3).reshape(4, 32, D)
        )
        fc2_shard = fc2_weight.reshape(4, 32, D)
        z0 = gather_z(jnp.concatenate([fc1_shard[:1], fc2_shard[:1]], axis=0))
        z1 = gather_z(after(jnp.concatenate([fc1_shard[1:], fc2_shard[1:]], axis=0), *z0))
        vec4 = jnp.concatenate([v[None] for v in gather_z(after(packed, *z0))], axis=0)
        za, zb = stack_z(z0, 0, 1), stack_z(z0, 1, 2)
        near_a = jnp.concatenate([za, send(za, y_way)], axis=0)
        near_b = jnp.concatenate([zb, send(zb, x_way)], axis=0)
        vec8 = jnp.concatenate([vec4, send(vec4, y_way)], axis=0)
        far_a, far_b = send(near_a, x_way), send(near_b, y_way)
        vec16 = jnp.concatenate([vec8, send(vec8, x_way)], axis=0)
        m0_a = (near_a, far_a, send(near_a, core), send(far_a, core))
        m0_b = (near_b, far_b, send(near_b, core), send(far_b, core))
        vec32 = jnp.concatenate([vec16, send(vec16, core)], axis=0)
        places = jnp.arange(32, dtype=jnp.int32)
        pick = (tab[None, :32] == places[:, None]).astype(BF)
        packed = mm(pick, vec32.reshape(32, -1))
    else:
        ident = jnp.arange(32, dtype=jnp.int32)
        tab = jnp.concatenate([ident, ident, ident[:16], ident[:16], ident[:1]])
        packed = lax.all_gather(packed, "fsdp", axis=0, tiled=True).reshape(devices, -1)
        packed = packed.astype(F32)
        fc1 = gather_any(fc1_weight.reshape(own_d, 4, D).transpose(1, 0, 2))
        fc2 = lax.all_gather(fc2_weight, "fsdp", axis=0, tiled=True)
        fc2 = in_pieces(fc2.reshape(4, 32, 32, D))
        m0_a, m1_a = tuple(w[:, :1] for w in fc1), tuple(w[:, 1:] for w in fc1)
        m0_b, m1_b = tuple(w[:, :1] for w in fc2), tuple(w[:, 1:] for w in fc2)
        t_a = gather_any(jnp.stack([q_w, dense_weight]))
        t_b = gather_any(jnp.stack([k_w, v_w]))

    full, at = [], 0
    for v in vectors:
        full.append(packed[:, at : at + v.shape[0]])
        at += v.shape[0]
    gain1, bias1, dense_b, gain2, bias2, fc2_b, qkv_b = [v.reshape(-1) for v in full[:7]]
    qkv_b = qkv_b.reshape(3, 1, D)
    if chips:
        fc1_b = full[7].reshape(32, 4, 32).transpose(1, 0, 2).reshape(4, 1, D)
    else:
        fc1_b = full[7].reshape(4, 1, D)

    if chips:
        tokens, out_cotangent, seq_lengths, seq_device, seq_offset = after(
            (tokens, out_cotangent, seq_lengths, seq_device, seq_offset), near_a, near_b
        )
    segment, position = locate(seq_lengths, seq_device, seq_offset, rows, which)
    tables = rotary_tables(position)
    rows_in = tokens.astype(F32)
    row_mean = jnp.mean(rows_in, axis=-1, keepdims=True)
    centred = rows_in - row_mean
    row_var = jnp.mean(centred * centred, axis=-1, keepdims=True)
    scale = lax.rsqrt(row_var + EPSILON)
    normal = centred * scale
    n1 = (normal * gain1 + bias1).astype(BF)
    n2 = (normal * gain2 + bias2).astype(BF)
    grad_out = out_cotangent.astype(F32)
    cotangent_sum = jnp.sum(grad_out, axis=0)
    g = out_cotangent
    seg_col, seg_row = segment[:, None], segment[None, :]

    def mlp(data, block, pieces, place, earlier):
        return mlp_part(
            tab, data, g, fc1_b[block : block + 1], *pieces, place, block % 2, 2, earlier
        )

    if chips:
        za, zb = after((stack_z(z1, 0, 3), stack_z(z1, 3, 6)), near_a, near_b)
        near_a = jnp.concatenate([za, send(za, y_way)], axis=0)
        near_b = jnp.concatenate([zb, send(zb, x_way)], axis=0)
        t_shards = after(jnp.stack([q_w, dense_weight, k_w, v_w]), near_a, near_b)
        start = after(n2, near_a, near_b, t_shards, n1, tables, seg_col, seg_row, qkv_b)
        r0 = mlp(start, 0, (m0_a, m0_b), 0, ())
        far_a, far_b = beside(near_a, x_way, r0), beside(near_b, y_way, r0)
        zt = gather_z(after(t_shards, far_a, far_b))
        m1_a = (near_a, far_a, send(near_a, core), send(far_a, core))
        m1_b = (near_b, far_b, send(near_b, core), send(far_b, core))
        r1 = mlp(after(n2, r0[4]), 1, (m1_a, m1_b), 0, r0[:4])
        zt = [zt[0], *after(zt[1:], r1[4])]
        za, zb = stack_z(zt, 0, 2), stack_z(zt, 2, 4)
        r2 = mlp(after(n2, za, zb, r1[4]), 2, (m1_a, m1_b), 1, ())
        near_a = jnp.concatenate([za, beside(za, y_way, r2)], axis=0)
        near_b = jnp.concatenate([zb, beside(zb, x_way, r2)], axis=0)
        got_a, got_b = beside(r1[1], core, r2), beside(r1[3], core, r2)
        r3 = mlp(after(n2, near_a, near_b, got_a, got_b, r2[4]), 3, (m1_a, m1_b), 2, r2[:4])
        far_a, far_b = beside(near_a, x_way, r3), beside(near_b, y_way, r3)
        t_a = (near_a, far_a, send(near_a, core), send(far_a, core))
        t_b = (near_b, far_b, send(near_b, core), send(far_b, core))
        keep = after((r1[0], r1[2]), r3[4])
        away_a, sum_a = scatter_one(keep[0], got_a)
        away_b, sum_b = scatter_one(keep[1], got_b)
        qkvd = project(tab, after(n1, away_a, away_b, r3[4]), g, qkv_b, tables, t_a, t_b)
        got_a, got_b = beside(away_a, x_way, [qkvd]), beside(away_b, y_way, [qkvd])
        far2_a, far2_b = beside(r3[1], core, [qkvd]), beside(r3[3], core, [qkvd])
        away_a, more_a = scatter_two(sum_a, got_a)
        away_b, more_b = scatter_two(sum_b, got_b)
        away2_a, sum2_a = scatter_one(r3[0], far2_a)
        away2_b, sum2_b = scatter_one(r3[2], far2_b)
        first = attention(
            seg_col, seg_row, tables, after(qkvd, away_a, away_b, away2_a, away2_b), 0, 4, ()
        )
        got_a, got_b = beside(away_a, y_way, first), beside(away_b, x_way, first)
        got2_a, got2_b = beside(away2_a, x_way, first), beside(away2_b, y_way, first)
        z_part = scatter_z(more_a, got_a, more_b, got_b)
        away2_a, more2_a = scatter_two(sum2_a, got2_a)
        away2_b, more2_b = scatter_two(sum2_b, got2_b)
        second = attention(
            seg_col, seg_row, tables, after(qkvd, away2_a, away2_b), 4, 4, first
        )
        mixed, dq, dk, dv = second
        got2_a, got2_b = beside(away2_a, y_way, second), beside(away2_b, x_way, second)
        z_part2 = scatter_z(more2_a, got2_a, more2_b, got2_b)
        z_mlp = lambda s: jnp.concatenate([z_part(s), z_part2(s)], axis=0)
        z_away = [z_mlp(s).astype(BF) for s in (1, 2, 3)]
        b1 = dense_value(tab, after(n1, z_away), g, mixed, dv, t_a, t_b)
        z_got = [beside(v, z_ways[s + 1], b1) for s, v in enumerate(z_away)]
        got_a, got_b = send(b1[1], core), send(b1[3], core)
        away_a, sum_a = scatter_one(b1[0], got_a)
        away_b, sum_b = scatter_one(b1[2], got_b)
        b2 = query_key(tab, after(n1, away_a, away_b), dq, dk, t_a, t_b)
        got_a, got_b = beside(away_a, x_way, b2), beside(away_b, y_way, b2)
        got2_a, got2_b = send(b2[1], core), send(b2[3], core)
        away2_a, sum2_a = scatter_one(b2[0], got2_a)
        away2_b, sum2_b = scatter_one(b2[2], got2_b)
        away_a, more_a = scatter_two(sum_a, got_a)
        away_b, more_b = scatter_two(sum_b, got_b)
        gn_parts = after(
            [b1[5], b2[4]] + [r[5] for r in (r0, r1, r2, r3)], away2_a, away2_b, away_a, away_b
        )
    else:
        r0 = mlp(n2, 0, (m0_a, m0_b), 0, ())
        r1 = mlp(n2, 1, (m1_a, m1_b), 0, r0[:4])
        r2 = mlp(n2, 2, (m1_a, m1_b), 1, ())
        r3 = mlp(n2, 3, (m1_a, m1_b), 2, r2[:4])
        qkvd = project(tab, n1, g, qkv_b, tables, t_a, t_b)
        first = attention(seg_col, seg_row, tables, qkvd, 0, 4, ())
        mixed, dq, dk, dv = attention(seg_col, seg_row, tables, qkvd, 4, 4, first)
        b1 = dense_value(tab, n1, g, mixed, dv, t_a, t_b)
        b2 = query_key(tab, n1, dq, dk, t_a, t_b)
        gn_parts = [b1[5], b2[4]] + [r[5] for r in (r0, r1, r2, r3)]

    gn_parts = [v.astype(F32) for v in gn_parts]
    gn1, gn2 = gn_parts[0] + gn_parts[1], sum(gn_parts[2:])
    out_parts = [b1[4], r0[4], r1[4], r2[4], r3[4]]
    grad_ln1_g = jnp.sum(gn1 * normal, axis=0)
    grad_ln1_b = jnp.sum(gn1, axis=0)
    grad_ln2_g = jnp.sum(gn2 * normal, axis=0)
    grad_ln2_b = jnp.sum(gn2, axis=0)
    gqkv_b = jnp.concatenate([b2[5], b1[6]], axis=0)
    gfc1_b = jnp.concatenate([r0[6], r1[6], r2[6], r3[6]], axis=0)[:, 0]
    if chips:
        gfc1_b = gfc1_b.reshape(4, 32, 32).transpose(1, 0, 2)
    small = [
        v.reshape(devices, -1)
        for v in (grad_ln1_g, grad_ln1_b, cotangent_sum, grad_ln2_g, grad_ln2_b, gqkv_b, gfc1_b)
    ]
    joint = jnp.concatenate(small, axis=1)
    if chips:
        j = places // 2
        slot = ((places % 2) ^ (which % 2)) * 16 + jnp.take(tab[64:80], j)
        to_slot = (slot[None, :] == places[:, None]).astype(F32)
        vec = jnp.dot(to_slot, joint, precision=lax.Precision.HIGHEST)
    if chips:
        got2_a, got2_b = send(away2_a, x_way), send(away2_b, y_way)
        away2_a, more2_a = scatter_two(sum2_a, got2_a)
        away2_b, more2_b = scatter_two(sum2_b, got2_b)
        got_a, got_b = send(away_a, y_way), send(away_b, x_way)
        z_b1 = scatter_z(more_a, got_a, more_b, got_b)
        got2_a, got2_b = send(away2_a, y_way), send(away2_b, x_way)
        z_b2 = scatter_z(more2_a, got2_a, more2_b, got2_b)
        z_back = lambda s: jnp.concatenate([z_b1(s), z_b2(s)], axis=0)
        z_away2 = [z_back(s).astype(BF) for s in (1, 2, 3)]
        out_parts = after(out_parts, z_away2)
        joint = after(vec, z_away2)
        joint = joint[:16] + send(joint[16:], core)
        joint = joint[:8] + send(joint[8:], x_way)
        joint = joint[:4] + send(joint[4:], y_way)
        owned = joint[0] + sum(send(joint[s], z_ways[s]) for s in (1, 2, 3))
    else:
        joint = jnp.pad(joint, ((0, 0), (0, -joint.shape[1] % 1024))).reshape(-1, 128)
        owned = lax.psum_scatter(joint, "fsdp", scatter_dimension=0, tiled=True).reshape(-1)
    out, at = [], 0
    for v in small:
        out.append(owned[at : at + v.shape[1]])
        at += v.shape[1]
    o_ln1_g, o_ln1_b, o_cot, o_ln2_g, o_ln2_b, o_qkv_b, o_fc1_b = out

    result = (rows_in + sum(v.astype(F32) for v in out_parts) + dense_b + fc2_b).astype(BF)
    into = gn1 * gain1 + gn2 * gain2
    if chips:
        into, part = after((into, z_mlp(0)), z_away2)
        part = part + sum(v.astype(F32) for v in z_got)
        own0, own1 = part[:4], part[4:]
        g_fc1 = jnp.concatenate([own0[:2], own1[:2]], axis=0)
        g_fc2 = jnp.concatenate([own0[2:], own1[2:]], axis=0)
        g_fc1 = g_fc1.reshape(4, 32, 32, 32).transpose(1, 2, 0, 3).reshape(32, FF)
        g_fc2 = g_fc2.reshape(128, D)
        own_b = z_back(0) + sum(
            send(v, z_ways[s + 1]).astype(F32) for s, v in enumerate(z_away2)
        )
        own_b1, own_b2 = own_b[:2], own_b[2:]
        g_t = (own_b2[0], own_b2[1], own_b1[1], own_b1[0])
    else:
        first, second = keep_whole(*r1[:4]), keep_whole(*r3[:4])
        g_fc1 = jnp.concatenate([first[0], second[0]], axis=0)
        g_fc2 = jnp.concatenate([first[1], second[1]], axis=0)
        g_fc1 = lax.psum_scatter(g_fc1, "fsdp", scatter_dimension=1, tiled=True)
        g_fc1 = g_fc1.transpose(1, 0, 2).reshape(own_d, FF)
        g_fc2 = lax.psum_scatter(
            g_fc2.reshape(FF, D), "fsdp", scatter_dimension=0, tiled=True
        )
        dense_part, value_part = keep_whole(*b1[:4])
        g_t = lax.psum_scatter(
            jnp.concatenate([*keep_whole(*b2[:4]), value_part, dense_part], axis=0),
            "fsdp", scatter_dimension=1, tiled=True,
        )
    g_qkv = jnp.concatenate(g_t[:3], axis=1)
    g_dense = g_t[3]

    back = scale * (
        into
        - jnp.mean(into, axis=-1, keepdims=True)
        - normal * jnp.mean(into * normal, axis=-1, keepdims=True)
    )
    grad_tokens = (grad_out + back).astype(BF)
    return (
        result, grad_tokens, o_ln1_g, o_ln1_b, g_qkv, o_qkv_b, g_dense, o_cot,
        o_ln2_g, o_ln2_b, g_fc1, o_fc1_b, g_fc2, o_cot,
    )


def solution(mesh):
    rows, vec, whole = P("fsdp", None), P("fsdp"), P()
    return jax.shard_map(
        partial(on_device, mesh.shape["fsdp"]),
        mesh=mesh,
        in_specs=(
            rows, rows, whole, whole, whole, vec, vec, rows, vec, rows, vec, vec, vec,
            rows, vec, rows, vec,
        ),
        out_specs=(
            rows, rows, vec, vec, rows, vec, rows, vec, vec, vec, rows, vec, rows, vec,
        ),
        check_vma=False,
    )
```
